512 devices in a mesh: gx: 16 (over z), gy: 4 (over x), gz: 8 (over y, core).
Axes of the slice: x: 4, y: 4, z: 16, core: 2. Of those that a mesh axis runs over, the one named last changes fastest.
Arguments:
- positions: float32 [3, 16, 4, 8, 1024], P(None, 'gx', 'gy', 'gz'), as said below
- velocities: float32 [3, 16, 4, 8, 1024], P(None, 'gx', 'gy', 'gz'), may hold values from -6 to 6
- radius: float32 [16, 4, 8, 1024], P('gx', 'gy', 'gz'), may hold values from 0.4 to 0.7
- group: int32 [16, 4, 8, 1024], P('gx', 'gy', 'gz'), may hold values from 0 to 1
- broken: int32 [16, 4, 8, 1024], P('gx', 'gy', 'gz'), may hold values 0 or 1
- cell: int32 [16, 4, 8, 1024], P('gx', 'gy', 'gz'), may hold values from 0 to 511
- neighbours: int32 [16, 4, 8, 8, 6], P('gx', 'gy', 'gz'), may hold values from 7 to 208, as said below
- counts: int32 [16, 4, 8, 8], P('gx', 'gy', 'gz'), may hold values from 2 to 6, as said below
Outputs:
- new_positions: float32 [3, 16, 4, 8, 1024], P(None, 'gx', 'gy', 'gz')
- new_velocities: float32 [3, 16, 4, 8, 1024], P(None, 'gx', 'gy', 'gz')
- smooth_stress: float32 [6, 128, 32, 64], P(None, 'gx', ('gy', 'gz'))
- smooth_motion: float32 [4, 128, 32, 64], P(None, 'gx', ('gy', 'gz'))
- energies: float32 [3], replicated
The draws below stay inside these ranges and needn't reach their ends.
Inputs may be any that keep to these rules, and one draw needn't show every extreme that they name: `positions`: particle p of brick (bx, by, bz) lies inside that brick's cube of edge e = 1024^(1/3), with its x coordinate between (bx + (p // 128) / 8) e and (bx + (p // 128 + 1) / 8) e. `neighbours`: a tile's slots name distinct tiles; for tile t each is tile t - 1, t or t + 1 of a brick at y and z offsets -1, 0, 1 and x offset 0, where t - 1 = -1 stands for tile 8 - 1 of the brick at x offset -1 and t + 1 = 8 for tile 0 of the brick at x offset 1. `counts`: some bricks have a tile whose list uses all 6 slots.
All inputs are finite; a program needn't handle non-finite values. No bound on the sum of `broken` on one device may be relied on, other than what follows from the above.
Results may differ from the reference program's by a relative error of at most 0.0003.
Values sent between devices are 32-bit elements; how exact they have to be, the bound alone decides.
No kernel may reach another device: no remote copies, remote signals or barrier semaphores. Data moves between devices by JAX's collectives and lax.ppermute only.
A program may use at most 64 MiB of HBM per device.

```python
import jax
import jax.numpy as jnp
from jax import lax

PB = 1024
NT = 8
K = 6
STEPS = 2
CX = 8
CY = 8
CZ = 8
SIGMA = 2
HW = 6
BRX = 16
BRY = 4
BRZ = 8


def draw_positions(key, part):
    key = jax.random.fold_in(key, 1)
    edge = float(PB) ** (1.0 / 3.0)
    inner = jax.random.uniform(key, (3, BRX, BRY, BRZ, PB), jnp.float32)
    tile_index = (lax.broadcasted_iota(jnp.int32, (BRX, BRY, BRZ, PB), 3) // 128).astype(jnp.float32)
    slab = (tile_index + inner[0]) / float(NT)
    inner = jnp.concatenate([slab[None], inner[1:3]], axis=0)
    anchor = jnp.stack([lax.broadcasted_iota(jnp.float32, (BRX, BRY, BRZ, PB), axis_number) for axis_number in range(3)])
    return (anchor + inner) * edge


def draw_velocities(key, part):
    key = jax.random.fold_in(key, 2)
    first_key, second_key = jax.random.split(key)
    ramp = 1.0 + 2.0 * lax.broadcasted_iota(jnp.float32, (BRX, BRY, BRZ, PB), 0) / max(BRX - 1, 1)
    noise = jnp.clip(0.3 * jax.random.normal(first_key, (3, BRX, BRY, BRZ, PB), jnp.float32), -1.2, 1.2)
    strike = jnp.ones((BRX, BRY, BRZ, PB), jnp.float32)
    zeros_plane = jnp.zeros((BRX, BRY, BRZ, PB), jnp.float32)
    return noise + jnp.stack([-ramp * strike, zeros_plane, zeros_plane])


def draw_counts(key, part):
    key = jax.random.fold_in(key, 3)
    drawn = jax.random.randint(key, (BRX, BRY, BRZ, NT), 2, K + 1)
    tile_index = lax.broadcasted_iota(jnp.int32, (BRX, BRY, BRZ, NT), 3)
    brick_sum = sum((lax.broadcasted_iota(jnp.int32, (BRX, BRY, BRZ, NT), axis_number) for axis_number in range(3)))
    full_tile = (tile_index == brick_sum % NT) & (brick_sum % 3 == 0)
    return jnp.where(full_tile, K, drawn).astype(jnp.int32)


def draw_neighbours(key, part):
    key = jax.random.fold_in(key, 4)
    candidate = lax.broadcasted_iota(jnp.int32, (BRX, BRY, BRZ, NT, 27), 4)
    scores = jax.random.randint(key, (BRX, BRY, BRZ, NT, 27), 0, 1 << 20) * 32 + candidate
    chosen = lax.top_k(scores, K)[1].astype(jnp.int32)
    step_x = chosen // 9 - 1
    step_y = chosen // 3 % 3 - 1
    step_z = chosen % 3 - 1
    tile_index = lax.broadcasted_iota(jnp.int32, (BRX, BRY, BRZ, NT, K), 3)
    moved = tile_index + step_x
    brick_x = jnp.where(moved < 0, -1, jnp.where(moved >= NT, 1, 0))
    target_tile = moved - brick_x * NT
    offset_index = ((brick_x + 1) * 3 + step_y + 1) * 3 + step_z + 1
    return (offset_index * NT + target_tile).astype(jnp.int32)


def touch_ends(entries, key, low, largest):
    spot = [jax.random.randint(jax.random.fold_in(key, axis), (), 0, length) for axis, length in enumerate(entries.shape)]
    longest = entries.shape.index(max(entries.shape))
    neighbour = spot[:longest] + [(spot[longest] + 1) % entries.shape[longest]] + spot[longest + 1:]
    return entries.at[tuple(spot)].set(low).at[tuple(neighbour)].set(largest)


def shard_levels(rng, shape, cuts, smallest, top_value):
    loudness, own = 1.0, jax.random.fold_in(rng, 6)
    for dim, blocks in cuts:
        heights = jnp.exp(jax.random.uniform(jax.random.fold_in(own, dim), (blocks,), jnp.float32, smallest / len(cuts), top_value / len(cuts)))
        loudness = loudness * jnp.repeat(heights, shape[dim] // blocks).reshape([-1 if axis == dim else 1 for axis in range(len(shape))])
    return loudness


def setup_inputs(seed: int = 0) -> dict:
    key_list = jax.random.split(jax.random.key(seed), 9)
    positions = draw_positions(jax.random.fold_in(key_list[8], 71), 0)
    velocities = draw_velocities(jax.random.fold_in(key_list[8], 71), 0)
    radius = jnp.clip(0.4 + 0.29999998 * jax.random.uniform(key_list[2], (BRX, BRY, BRZ, PB), jnp.float32) ** shard_levels(key_list[2], (BRX, BRY, BRZ, PB), ((0, 16), (1, 4), (2, 8)), -0.2, 0.2), 0.4, 0.7)
    group = touch_ends(jax.random.randint(key_list[3], (BRX, BRY, BRZ, PB), 0, 2), jax.random.fold_in(key_list[3], 1), 0, 1).astype(jnp.int32)
    broken = touch_ends((jax.random.randint(key_list[4], (BRX, BRY, BRZ, PB), 0, 4) < 1).astype(jnp.int32), jax.random.fold_in(key_list[4], 1), 0, 1)
    cell = touch_ends(jax.random.randint(key_list[5], (BRX, BRY, BRZ, PB), 0, CX * CY * CZ), jax.random.fold_in(key_list[5], 1), 0, (CX * CY * CZ) - 1).astype(jnp.int32)
    neighbours = draw_neighbours(jax.random.fold_in(key_list[8], 71), 0)
    counts = draw_counts(jax.random.fold_in(key_list[8], 71), 0)
    return dict(positions=positions, velocities=velocities, radius=radius, group=group, broken=broken, cell=cell, neighbours=neighbours, counts=counts)


KN = 1.0
GAMMA = 1.0
KB = 2.0
REACH = 1.5
STEP_DT = 0.02
DENS = 4.0
SOFT = 0.0001

def pair_terms(own_tile, partner, live_mask, bond_mask):
    offsets = partner[0:3, :, None, :] - own_tile[0:3, :, :, None]
    distance = jnp.sqrt(lax.optimization_barrier(jnp.sum(offsets * offsets, axis=0)) + SOFT)
    direction = offsets / distance
    contact_reach = own_tile[6][:, :, None] + partner[6][:, None, :]
    intersection = jnp.maximum(contact_reach - distance, 0.0) * live_mask
    closing = lax.optimization_barrier(jnp.sum((partner[3:6, :, None, :] - own_tile[3:6, :, :, None]) * direction, axis=0))
    intersection_root = jnp.sqrt(intersection)
    window = jnp.maximum(1.0 - distance / (REACH * contact_reach), 0.0)
    window = window * window * bond_mask
    stretch = distance - contact_reach
    magnitude = -KN * intersection * intersection_root + GAMMA * intersection_root * closing + KB * stretch * window
    force = lax.optimization_barrier(jnp.sum(magnitude[None] * direction, axis=3))
    scaled = -0.5 * magnitude / distance
    component_pairs = [(0, 0), (1, 1), (2, 2), (0, 1), (0, 2), (1, 2)]
    virial = jnp.stack([lax.optimization_barrier(jnp.sum(scaled * offsets[first] * offsets[second], axis=2)) for first, second in component_pairs])
    contact_energy = lax.optimization_barrier(jnp.sum(0.4 * KN * intersection * intersection * intersection_root, axis=2))
    bond_energy = lax.optimization_barrier(jnp.sum(0.5 * KB * stretch * stretch * window, axis=2))
    return (force, virial, contact_energy, bond_energy)

def brick_forces(tiles, neighbour_list, listed, group_tiles, broken_tiles):
    tile_count = neighbour_list.shape[0]
    slots = neighbour_list.shape[1]
    centre = 13 * tile_count
    own_tile = tiles[:, centre:centre + tile_count, :]
    lanes = jnp.arange(128)
    diagonal = lanes[:, None] == lanes[None, :]
    keeping = 1.0 - broken_tiles.astype(jnp.float32)
    tile_ids = jnp.arange(tile_count).astype(jnp.int32)

    def visit(column, carried):
        picked = neighbour_list[:, column]
        partner = jnp.take(tiles, picked, axis=1)
        active = (column < listed).astype(jnp.float32)
        relative = picked - centre
        inside = ((relative >= 0) & (relative < tile_count)).astype(jnp.float32)
        position_slot = jnp.clip(relative, 0, tile_count - 1)
        itself = ((relative == tile_ids)[:, None, None] & diagonal[None]).astype(jnp.float32)
        present = (partner[6] > 0).astype(jnp.float32)
        live_mask = active[:, None, None] * present[:, None, :] * (1.0 - itself)
        partner_group = jnp.take(group_tiles, position_slot, axis=0)
        partner_keep = jnp.take(keeping, position_slot, axis=0)
        same_group = (group_tiles[:, :, None] == partner_group[:, None, :]).astype(jnp.float32)
        bond_mask = live_mask * inside[:, None, None] * same_group * keeping[:, :, None] * partner_keep[:, None, :]
        terms = pair_terms(own_tile, partner, live_mask, bond_mask)
        return tuple((previous + added for previous, added in zip(carried, terms)))
    starting = (jnp.zeros((3, tile_count, 128), jnp.float32), jnp.zeros((6, tile_count, 128), jnp.float32), jnp.zeros((tile_count, 128), jnp.float32), jnp.zeros((tile_count, 128), jnp.float32))
    return lax.fori_loop(0, slots, visit, starting)

def gauss_table():
    offset_cells = jnp.arange(-HW, HW + 1).astype(jnp.float32)
    raw_weights = jnp.exp(-offset_cells * offset_cells / (2.0 * SIGMA * SIGMA))
    return raw_weights / jnp.sum(raw_weights)

def smooth_axis(field, axis_number):
    weights = gauss_table()
    length = field.shape[axis_number]
    padding = [(0, 0)] * field.ndim
    padding[axis_number] = (HW, HW)
    padded = jnp.pad(field, padding)
    total = jnp.zeros(field.shape, jnp.float32)
    for offset_index in range(2 * HW + 1):
        total = total + weights[offset_index] * lax.slice_in_dim(padded, offset_index, offset_index + length, axis=axis_number)
    return total

def neighbour_tiles(state):
    count_x, count_y, count_z, width = state.shape[1:]
    padded = jnp.pad(state, ((0, 0), (1, 1), (1, 1), (1, 1), (0, 0)))
    pieces = []
    for first in range(3):
        for second in range(3):
            for third in range(3):
                pieces.append(padded[:, first:first + count_x, second:second + count_y, third:third + count_z, :])
    stacked = jnp.stack(pieces, axis=4)
    stacked = stacked.reshape(7, count_x * count_y * count_z, 27 * width // 128, 128)
    return jnp.moveaxis(stacked, 1, 0)

def reference(positions, velocities, radius, group, broken, cell, neighbours, counts):
    count_x, count_y, count_z, width = radius.shape
    tile_count = width // 128
    bricks = count_x * count_y * count_z
    state = jnp.concatenate([positions, velocities, radius[None]], axis=0)
    group_tiles = group.reshape(bricks, tile_count, 128)
    broken_tiles = broken.reshape(bricks, tile_count, 128)
    lists = neighbours.reshape(bricks, tile_count, K)
    listed = counts.reshape(bricks, tile_count)
    mass = DENS * radius * radius * radius

    def per_brick(packed):
        return brick_forces(packed[0], packed[1], packed[2], packed[3], packed[4])
    for repeat in range(STEPS):
        tiles = neighbour_tiles(state)
        force, virial, contact, bonding = lax.map(per_brick, (tiles, lists, listed, group_tiles, broken_tiles))
        force = jnp.moveaxis(force.reshape(bricks, 3, width), 0, 1).reshape(3, count_x, count_y, count_z, width)
        speed = state[3:6] + STEP_DT * force / mass
        place = state[0:3] + STEP_DT * speed
        state = jnp.concatenate([place, speed, state[6:7]], axis=0)
    speed = state[3:6]
    kinetic = 0.5 * mass * lax.optimization_barrier(jnp.sum(speed * speed, axis=0))
    scale = float(CX * CY * CZ) / float(PB)
    momentum = jnp.moveaxis((mass * speed).reshape(3, bricks, width), 1, 0)
    values = jnp.concatenate([virial.reshape(bricks, 6, width), momentum, kinetic.reshape(bricks, 1, width)], axis=1) * scale
    cells_flat = cell.reshape(bricks, width)

    def deposit_one(brick_values, brick_cells):
        return jax.ops.segment_sum(brick_values.T, brick_cells, num_segments=CX * CY * CZ).T
    deposit = jax.vmap(deposit_one)(values, cells_flat)
    deposit = deposit.reshape(count_x, count_y, count_z, 10, CX, CY, CZ)
    deposit = jnp.transpose(deposit, (3, 0, 4, 1, 5, 2, 6)).reshape(10, count_x * CX, count_y * CY, count_z * CZ)
    field = smooth_axis(deposit, 2)
    field = smooth_axis(field, 3)
    field = smooth_axis(field, 1)
    energies = jnp.stack([jnp.sum(kinetic), jnp.sum(contact), jnp.sum(bonding)])
    return (state[0:3], state[3:6], field[0:6], field[6:10], energies)
```

```python
import math

import jax
import jax.numpy as jnp
from jax import lax
from jax.experimental import pallas as pl
from jax.experimental.pallas import tpu as pltpu
from jax.sharding import PartitionSpec as P

STEPS = 2
CX = 8
CY = 8
CZ = 8
SIGMA = 2
HW = 6
KN = 1.0
GAMMA = 1.0
KB = 2.0
REACH = 1.5
STEP_DT = 0.02
DENS = 4.0
SOFT = 0.0001

NT = 8
K = 6
FAR = -1.0e9
LIVE = 1024
INSIDE = 2048
ITSELF = 4096
COMPS = 10
VMEM = pl.BlockSpec(memory_space=pltpu.VMEM)
SMEM = pl.BlockSpec(memory_space=pltpu.SMEM)

RAW = [math.exp(-d * d / (2.0 * SIGMA * SIGMA)) for d in range(HW + 1)]
TOTAL = RAW[0] + 2.0 * sum(RAW[1:])
GAUSS = [w / TOTAL for w in RAW]


def row(tile, index):
    return jnp.broadcast_to(tile[index : index + 1, :], (8, 128))


def pair_sums(tiles, meta, base, own, second):
    xi, yi, zi = row(own, 0), row(own, 1), row(own, 2)
    ui, vi, wi = row(own, 3), row(own, 4), row(own, 5)
    ri = row(own, 6)
    sub = lax.broadcasted_iota(jnp.int32, (8, 128), 0)
    lane = lax.broadcasted_iota(jnp.int32, (8, 128), 1)
    zero = jnp.zeros((8, 128), jnp.float32)
    count = 10 if second else 3
    sums = [zero] * count
    for slot in range(K):
        entry = meta[base + slot]
        partner = tiles[lax.bitwise_and(entry, 1023)]
        live = lax.bitwise_and(entry, LIVE) > 0
        dead = jnp.logical_and(sub == 6, jnp.logical_or(partner <= 0.0, jnp.logical_not(live)))
        partner = jnp.where(dead, FAR, partner)
        columns = partner.T
        if second:
            selfrow = jnp.where(lax.bitwise_and(entry, ITSELF) > 0, lane, -1)
        for chunk in range(16):
            part = columns[8 * chunk : 8 * chunk + 8, :]
            col = [jnp.broadcast_to(part[:, c : c + 1], (8, 128)) for c in range(7)]
            dx, dy, dz = col[0] - xi, col[1] - yi, col[2] - zi
            square = dx * dx + dy * dy + (dz * dz + SOFT)
            inverse = lax.rsqrt(square)
            inter = jnp.maximum((col[6] + ri) - square * inverse, 0.0)
            root = inter * lax.rsqrt(jnp.maximum(inter, 1e-30))
            closing = ((col[3] - ui) * dx + (col[4] - vi) * dy + (col[5] - wi) * dz) * inverse
            scaled = root * (GAMMA * closing - KN * inter) * inverse
            fx, fy, fz = scaled * dx, scaled * dy, scaled * dz
            sums[0] = sums[0] + fx
            sums[1] = sums[1] + fy
            sums[2] = sums[2] + fz
            if second:
                sums[3] = sums[3] + fx * dx
                sums[4] = sums[4] + fy * dy
                sums[5] = sums[5] + fz * dz
                sums[6] = sums[6] + fx * dy
                sums[7] = sums[7] + fx * dz
                sums[8] = sums[8] + fy * dz
                energy = inter * inter * root
                sums[9] = sums[9] + jnp.where(sub + 8 * chunk == selfrow, 0.0, energy)
    return sums


def bond_sums(tiles, entry, own, second, sums):
    xi, yi, zi, ri = row(own, 0), row(own, 1), row(own, 2), row(own, 6)
    code = row(own, 7)
    code = jnp.where(code < 0.0, -5.0, code)
    sub = lax.broadcasted_iota(jnp.int32, (8, 128), 0)
    lane = lax.broadcasted_iota(jnp.int32, (8, 128), 1)
    partner = tiles[lax.bitwise_and(entry, 1023)]
    columns = partner.T
    selfrow = jnp.where(lax.bitwise_and(entry, ITSELF) > 0, lane, -1)
    held = [sums[i] for i in range(11 if second else 3)]
    for chunk in range(16):
        part = columns[8 * chunk : 8 * chunk + 8, :]
        xj, yj, zj, rj, cj = [
            jnp.broadcast_to(part[:, c : c + 1], (8, 128)) for c in (0, 1, 2, 6, 7)
        ]
        dx, dy, dz = xj - xi, yj - yi, zj - zi
        square = dx * dx + dy * dy + (dz * dz + SOFT)
        inverse = lax.rsqrt(square)
        distance = square * inverse
        reach = rj + ri
        bonded = jnp.logical_and(cj == code, sub + 8 * chunk != selfrow)
        bonded = jnp.logical_and(bonded, rj > 0.0)
        window = jnp.maximum(1.0 - distance / (REACH * reach), 0.0)
        window = jnp.where(bonded, window * window, 0.0)
        stretch = distance - reach
        pull = stretch * window
        scaled = KB * pull * inverse
        fx, fy, fz = scaled * dx, scaled * dy, scaled * dz
        held[0] = held[0] + fx
        held[1] = held[1] + fy
        held[2] = held[2] + fz
        if second:
            held[3] = held[3] + fx * dx
            held[4] = held[4] + fy * dy
            held[5] = held[5] + fz * dz
            held[6] = held[6] + fx * dy
            held[7] = held[7] + fx * dz
            held[8] = held[8] + fy * dz
            held[10] = held[10] + pull * stretch
    for i, value in enumerate(held):
        sums[i] = value


def tile_sums(tiles, meta, base, own, second, sums):
    for i, value in enumerate(pair_sums(tiles, meta, base, own, second)):
        sums[i] = value
    if second:
        sums[10] = jnp.zeros((8, 128), jnp.float32)

    @pl.loop(0, K)
    def _(slot):
        entry = meta[base + slot]

        @pl.when(lax.bitwise_and(entry, INSIDE) > 0)
        def _():
            bond_sums(tiles, entry, own, second, sums)


def folded(value):
    return jnp.sum(value, axis=0, keepdims=True)


def fill(tiles, low, middle, high, size):
    for part, ref in enumerate((low, middle, high)):
        for i in range(size):
            tiles[part * size + i] = ref[i]


def first_kernel(meta, low, middle, high, out, tiles, sums):
    width = middle.shape[0] // 3
    fill(tiles, low, middle, high, 3 * width)
    sub = lax.broadcasted_iota(jnp.int32, (8, 128), 0)

    @pl.loop(0, width - 2)
    def _(t):
        own = tiles[4 * width + t + 1]
        tile_sums(tiles, meta, t * 8, own, False, sums)
        radius = own[6:7, :]
        gain = STEP_DT / (DENS * radius * radius * radius)
        fresh = own
        for axis in range(3):
            speed = own[3 + axis : 4 + axis, :] + gain * folded(sums[axis])
            place = own[axis : axis + 1, :] + STEP_DT * speed
            fresh = jnp.where(sub == axis, place, fresh)
            fresh = jnp.where(sub == 3 + axis, speed, fresh)
        out[t] = fresh


def second_kernel(
    meta, cell, low, middle, high, place_out, speed_out, grid_out, energy_out, tiles, sums, left, right, total
):
    width = middle.shape[0] // 3
    fill(tiles, low, middle, high, 3 * width)
    sub = lax.broadcasted_iota(jnp.int32, (8, 128), 0)
    line = lax.broadcasted_iota(jnp.int32, (64, 128), 0)
    total[...] = jnp.zeros((8, 128), jnp.float32)
    right[...] = jnp.zeros(right.shape, jnp.bfloat16)

    for t in range(NT):
        own = tiles[4 * width + t + 1]
        tile_sums(tiles, meta, t * 8, own, True, sums)
        radius = own[6:7, :]
        mass = DENS * radius * radius * radius
        gain = STEP_DT / mass
        values = [-0.5 * folded(sums[3 + i]) for i in range(6)]
        squares = jnp.zeros((1, 128), jnp.float32)
        for axis in range(3):
            speed = own[3 + axis : 4 + axis, :] + gain * folded(sums[axis])
            speed_out[axis, t : t + 1, :] = speed
            place_out[axis, t : t + 1, :] = own[axis : axis + 1, :] + STEP_DT * speed
            squares = squares + speed * speed
            values.append(mass * speed)
        kinetic = 0.5 * mass * squares
        values.append(kinetic)
        contact = 0.4 * KN * folded(sums[9])
        bond = 0.5 * KB * folded(sums[10])
        added = jnp.where(sub == 0, kinetic, jnp.where(sub == 1, contact, jnp.where(sub == 2, bond, 0.0)))
        total[...] = total[...] + added
        where = cell[t : t + 1, :]
        span = slice(128 * t, 128 * t + 128)
        in_plane = sub == lax.shift_right_logical(where, 6)
        for c in range(0, COMPS, 2):
            pair = jnp.concatenate(
                [jnp.where(in_plane, values[c], 0.0), jnp.where(in_plane, values[c + 1], 0.0)], axis=0
            )
            coarse = pair.astype(jnp.bfloat16)
            fine = (pair - coarse.astype(jnp.float32)).astype(jnp.bfloat16)
            right[8 * c : 8 * c + 16, span] = coarse
            right[128 + 8 * c : 128 + 8 * c + 16, span] = fine
        left[:, span] = jnp.where(line == lax.bitwise_and(where, 63), 1.0, 0.0).astype(jnp.bfloat16)

    both = lax.dot_general(
        left[...], right[...], (((1,), (1,)), ((), ())), preferred_element_type=jnp.float32
    )
    scale = float(CX * CY * CZ) / float(NT * 128)
    grid_out[...] = (both[:, 0:128] + both[:, 128:256]) * scale
    for i in range(energy_out.shape[0]):
        energy_out[i] = total[...]


def plane_kernel(coords, own, before, after, energy, out):
    lane = lax.broadcasted_iota(jnp.int32, (8, 128), 1)
    inner = lax.bitwise_and(lane, 7)
    sums = energy[0]
    for i in range(1, energy.shape[0]):
        sums = sums + energy[i]
    sums = jnp.where(lane == 8 * COMPS, jnp.sum(sums, axis=1, keepdims=True), 0.0)
    planes = []
    for y in range(CY):
        block = slice(8 * y, 8 * y + 8)
        here = own[block, :]
        low = pltpu.roll(before[block, :], 120, 1)
        high = pltpu.roll(after[block, :], 8, 1)
        smooth = GAUSS[0] * here
        for d in range(1, HW + 1):
            ahead = pltpu.roll(jnp.where(inner >= d, here, high), 128 - d, 1)
            behind = pltpu.roll(jnp.where(inner < 8 - d, here, low), d, 1)
            smooth = smooth + GAUSS[d] * (ahead + behind)
        planes.append(smooth)
    rows = out.shape[0]
    for j in range(rows):
        out[j] = sums
    start = coords[1] * CY
    for r in range(-HW, CY + HW):
        mixed = sums
        for y in range(CY):
            if abs(r - y) <= HW:
                mixed = mixed + GAUSS[abs(r - y)] * planes[y]

        @pl.when(jnp.logical_and(start + r >= 0, start + r < rows))
        def _():
            out[start + r] = mixed


def line_kernel(parts, stress, motion, energies):
    count = parts.shape[0] // 8
    lane = lax.broadcasted_iota(jnp.int32, (8, 128), 1)
    sub = lax.broadcasted_iota(jnp.int32, (8, 128), 0)
    lines = []
    for block in range(8):
        line = parts[block]
        for other in range(1, count):
            line = line + parts[8 * other + block]
        lines.append(line)
    whole = lines[0]
    for line in lines[1:]:
        whole = whole + line
    for i in range(3):
        energies[i] = jnp.sum(jnp.where(jnp.logical_and(sub == i, lane == 8 * COMPS), whole, 0.0))
    empty = jnp.zeros((8, 128), jnp.float32)
    out = []
    for block in range(8):
        here = lines[block]
        low = lines[block - 1] if block > 0 else empty
        high = lines[block + 1] if block < 7 else empty
        smooth = GAUSS[0] * here
        for d in range(1, HW + 1):
            ahead = pltpu.roll(jnp.where(sub >= d, here, high), 8 - d, 0)
            behind = pltpu.roll(jnp.where(sub < 8 - d, here, low), d, 0)
            smooth = smooth + GAUSS[d] * (ahead + behind)
        out.append(smooth)
    turned = jnp.concatenate(out, axis=0).T
    for c in range(6):
        stress[c] = turned[8 * c : 8 * c + 8, :]
    for c in range(4):
        motion[c] = turned[48 + 8 * c : 56 + 8 * c, :]


def pack_kernel(place, speed, radius, group, broken, lists, counts, out, to_left, to_right):
    code = jnp.where(broken[...] == 0, group[...].astype(jnp.float32), -1.0)
    for t in range(NT):
        for axis in range(3):
            out[t, axis : axis + 1, :] = place[axis, t : t + 1, :]
            out[t, 3 + axis : 4 + axis, :] = speed[axis, t : t + 1, :]
        out[t, 6:7, :] = radius[t : t + 1, :]
        out[t, 7:8, :] = code[t : t + 1, :]
    for ref, edge, first in ((to_left, 0, 0), (to_right, NT - 1, NT - 2)):
        ref[0] = out[first]
        ref[1] = out[first + 1]
        ref[2] = jnp.zeros((8, 128), jnp.float32)
        ref[2, 0:1, 0:K] = lists[edge : edge + 1, :].astype(jnp.float32)
        ref[2, 1:2, 0:NT] = counts[...].astype(jnp.float32)


def shifted(value, axis, step, wrap):
    count = lax.axis_size(axis)
    pairs = [(i, (i + step) % count) for i in range(count) if wrap or 0 <= i + step < count]
    return lax.ppermute(value, axis, pairs)


def list_entries(lists, counts, home, shift, width, margin):
    offset = lists // NT
    along = offset // 9 - 1
    across = offset // 3 % 3
    up = offset % 3
    spot = jnp.clip((along + shift) * NT + lists % NT + margin, 0, width - 1)

    def within(axis, step):
        moved = lax.axis_index(axis) + step
        return (moved >= 0) & (moved < lax.axis_size(axis))

    live = lax.broadcasted_iota(jnp.int32, lists.shape, 1) < counts
    live = live & within("gx", shift) & within("gx", shift + along)
    live = live & within("gy", across - 1) & within("gz", up - 1)
    inside = live & (offset == 13)
    itself = inside & (spot == home)
    entry = up * (3 * width) + across * width + spot
    entry = entry + LIVE * live.astype(jnp.int32) + INSIDE * inside.astype(jnp.int32)
    entry = entry + ITSELF * itself.astype(jnp.int32)
    return jnp.pad(entry, ((0, 0), (0, 8 - K))).reshape(-1)


def shards(positions, velocities, radius, group, broken, cell, neighbours, counts):
    lists = neighbours.reshape(NT, K)
    listed = counts.reshape(1, NT)
    tile = jax.ShapeDtypeStruct((NT, 8, 128), jnp.float32)
    edge = jax.ShapeDtypeStruct((3, 8, 128), jnp.float32)
    own, to_left, to_right = pl.pallas_call(
        pack_kernel,
        out_shape=(tile, edge, edge),
        in_specs=[VMEM] * 7,
        out_specs=(VMEM, VMEM, VMEM),
        name="pack",
    )(
        positions.reshape(3, NT, 128),
        velocities.reshape(3, NT, 128),
        radius.reshape(NT, 128),
        group.reshape(NT, 128),
        broken.reshape(NT, 128),
        lists,
        listed,
    )
    from_left = shifted(to_right, "gx", 1, True)
    from_right = shifted(to_left, "gx", -1, True)
    line = jnp.concatenate([from_left[0:2], own, from_right[0:2]], axis=0)
    width = NT + 4

    def extended(tiles):
        up = shifted(tiles, "gy", 1, False)
        down = shifted(tiles, "gy", -1, False)
        middle = jnp.concatenate([up, tiles, down], axis=0)
        low = shifted(middle, "gz", 1, True)
        high = shifted(middle, "gz", -1, True)
        return low, middle, high

    low, middle, high = extended(line)
    all_lists = jnp.concatenate(
        [from_left[2, 0:1, 0:K].astype(jnp.int32), lists, from_right[2, 0:1, 0:K].astype(jnp.int32)], axis=0
    )
    all_counts = jnp.concatenate(
        [from_left[2, 1, NT - 1 : NT].astype(jnp.int32), listed[0], from_right[2, 1, 0:1].astype(jnp.int32)]
    )
    spots = lax.broadcasted_iota(jnp.int32, (NT + 2, 1), 0)
    shift = jnp.where(spots == 0, -1, jnp.where(spots == NT + 1, 1, 0))
    first_meta = list_entries(all_lists, all_counts[:, None], spots + 1, shift, width, 2)
    spots = lax.broadcasted_iota(jnp.int32, (NT, 1), 0)
    second_meta = list_entries(lists, listed.reshape(NT, 1), spots + 1, 0, width - 2, 1)

    line = pl.pallas_call(
        first_kernel,
        out_shape=jax.ShapeDtypeStruct((width - 2, 8, 128), jnp.float32),
        in_specs=[SMEM] + [VMEM] * 3,
        out_specs=VMEM,
        scratch_shapes=[
            pltpu.VMEM((9 * width, 8, 128), jnp.float32),
            pltpu.VMEM((11, 8, 128), jnp.float32),
        ],
        name="first_step",
    )(first_meta, low, middle, high)
    low, middle, high = extended(line)
    width = width - 2
    peers = lax.axis_size("gx")
    block = jax.ShapeDtypeStruct((3, NT, 128), jnp.float32)
    places, speeds, grid, energy = pl.pallas_call(
        second_kernel,
        out_shape=(
            block,
            block,
            jax.ShapeDtypeStruct((64, 128), jnp.float32),
            jax.ShapeDtypeStruct((peers, 8, 128), jnp.float32),
        ),
        in_specs=[SMEM] + [VMEM] * 4,
        out_specs=(VMEM,) * 4,
        scratch_shapes=[
            pltpu.VMEM((9 * width, 8, 128), jnp.float32),
            pltpu.VMEM((11, 8, 128), jnp.float32),
            pltpu.VMEM((64, NT * 128), jnp.bfloat16),
            pltpu.VMEM((256, NT * 128), jnp.bfloat16),
            pltpu.VMEM((8, 128), jnp.float32),
        ],
        name="second_step",
    )(second_meta, cell.reshape(NT, 128), low, middle, high)
    energy = lax.all_to_all(energy, "gx", 0, 0, tiled=True)
    before = shifted(grid, "gx", 1, False)
    after = shifted(grid, "gx", -1, False)
    coords = jnp.stack([lax.axis_index(a) for a in ("gx", "gy", "gz")])
    rows = lax.axis_size("gy") * lax.axis_size("gz")
    parts = pl.pallas_call(
        plane_kernel,
        out_shape=jax.ShapeDtypeStruct((rows, 8, 128), jnp.float32),
        in_specs=[SMEM] + [VMEM] * 4,
        out_specs=VMEM,
        name="planes",
    )(coords, grid, before, after, energy)
    parts = lax.all_to_all(parts, ("gy", "gz"), 0, 0, tiled=True)
    stress, motion, energies = pl.pallas_call(
        line_kernel,
        out_shape=(
            jax.ShapeDtypeStruct((6, 8, 64), jnp.float32),
            jax.ShapeDtypeStruct((4, 8, 64), jnp.float32),
            jax.ShapeDtypeStruct((3,), jnp.float32),
        ),
        in_specs=[VMEM],
        out_specs=(VMEM, VMEM, SMEM),
        name="lines",
    )(parts)
    return (
        places.reshape(positions.shape),
        speeds.reshape(velocities.shape),
        stress.reshape(6, CX, 1, 64),
        motion.reshape(4, CX, 1, 64),
        energies,
    )


def solution(mesh):
    placed = (
        P(None, "gx", "gy", "gz", None),
        P(None, "gx", "gy", "gz", None),
        P("gx", "gy", "gz", None),
        P("gx", "gy", "gz", None),
        P("gx", "gy", "gz", None),
        P("gx", "gy", "gz", None),
        P("gx", "gy", "gz", None, None),
        P("gx", "gy", "gz", None),
    )
    return jax.shard_map(
        shards,
        mesh=mesh,
        in_specs=placed,
        out_specs=(
            P(None, "gx", "gy", "gz", None),
            P(None, "gx", "gy", "gz", None),
            P(None, "gx", ("gy", "gz"), None),
            P(None, "gx", ("gy", "gz"), None),
            P(),
        ),
        check_vma=False,
    )
```

```python
import math

import jax
import jax.numpy as jnp
from jax import lax
from jax.experimental import pallas as pl
from jax.experimental.pallas import tpu as pltpu
from jax.sharding import PartitionSpec as P

STEPS = 2
CX = 8
CY = 8
CZ = 8
SIGMA = 2
HW = 6
KN = 1.0
GAMMA = 1.0
KB = 2.0
REACH = 1.5
STEP_DT = 0.02
DENS = 4.0
SOFT = 0.0001

NT = 8
K = 6
FAR = -1.0e9
LIVE = 1024
INSIDE = 2048
ITSELF = 4096
COMPS = 10
VMEM = pl.BlockSpec(memory_space=pltpu.VMEM)
SMEM = pl.BlockSpec(memory_space=pltpu.SMEM)

RAW = [math.exp(-d * d / (2.0 * SIGMA * SIGMA)) for d in range(HW + 1)]
TOTAL = RAW[0] + 2.0 * sum(RAW[1:])
GAUSS = [w / TOTAL for w in RAW]


def twice(value):
    return jnp.concatenate([value, value], axis=0)


def parts_of(value, count):
    parts = []
    for _ in range(count):
        part = value.astype(jnp.bfloat16)
        parts.append(part)
        value = value - part.astype(jnp.float32)
    return parts


def selector():
    shape = (32, 8 * 128)
    line = lax.broadcasted_iota(jnp.int32, shape, 0)
    block = lax.shift_right_logical(lax.broadcasted_iota(jnp.int32, shape, 1), 7)
    hit = jnp.logical_and(lax.bitwise_and(line, 7) == block, line < 24)
    return jnp.where(hit, 1.0, 0.0).astype(jnp.bfloat16)


def own_columns(own, select, mine):
    stack = jnp.concatenate(
        [part.astype(jnp.float32) for part in parts_of(own, 3)] + [jnp.zeros((8, 128), jnp.float32)], axis=0
    ).astype(jnp.bfloat16)
    wide = lax.dot_general(
        stack, select[...], (((0,), (0,)), ((), ())), preferred_element_type=jnp.float32
    )
    for c in range(8):
        mine[c] = wide[:, 128 * c : 128 * c + 128]


def pair_sums(tiles, meta, base, own, second, select, rows, mine):
    lane = lax.broadcasted_iota(jnp.int32, (8, 128), 1).astype(jnp.float32)
    for slot in range(K):
        entry = meta[base + slot]
        index = lax.bitwise_and(entry, 1023)
        live = lax.bitwise_and(entry, LIVE) > 0
        for c in range(8 if slot < 3 else 7):
            value = jnp.broadcast_to(tiles[index, c : c + 1, :], (8, 128))
            if c == 6:
                value = jnp.where(jnp.logical_and(live, value > 0.0), value, FAR)
            if c == 7:
                value = jnp.where(lax.bitwise_and(entry, INSIDE) > 0, value, -7.0)
            rows[9 * slot + c] = value
        if second and slot < 3:
            rows[9 * slot + 8] = jnp.where(lax.bitwise_and(entry, ITSELF) > 0, lane, -1.0)
    own_columns(own, select, mine)
    number = lax.broadcasted_iota(jnp.int32, (16, 128), 0).astype(jnp.float32)
    whole_lane = twice(lane)
    ones = jnp.ones((256, 128), jnp.bfloat16)
    count = 11 if second else 3
    totals = [jnp.zeros((16, 128), jnp.float32)] * count
    for block in range(8):
        xi, yi, zi, ui, vi, wi, ri, ci = [mine[c, 16 * block : 16 * block + 16, :] for c in range(8)]
        ci = jnp.where(ci < 0.0, -5.0, ci)
        here = number + float(16 * block)
        added = [jnp.zeros((16, 128), jnp.float32)] * count
        for slot in range(K):
            xj, yj, zj, uj, vj, wj, rj = [twice(rows[9 * slot + c]) for c in range(7)]
            dx, dy, dz = xj - xi, yj - yi, zj - zi
            square = dx * dx + dy * dy + (dz * dz + SOFT)
            inverse = lax.rsqrt(square)
            distance = square * inverse
            reach = rj + ri
            inter = jnp.maximum(reach - distance, 0.0)
            root = inter * lax.rsqrt(jnp.maximum(inter, 1e-30))
            closing = ((uj - ui) * dx + (vj - vi) * dy + (wj - wi) * dz) * inverse
            magnitude = root * (closing - inter)
            if slot < 3:
                ratio = lax.rsqrt(reach)
                window = jnp.maximum(1.0 - distance * ((1.0 / REACH) * ratio * ratio), 0.0)
                window = jnp.where(twice(rows[9 * slot + 7]) == ci, window * window, 0.0)
                stretch = distance - reach
                pull = stretch * window
                magnitude = magnitude + KB * pull
            scaled = magnitude * inverse
            fx, fy, fz = scaled * dx, scaled * dy, scaled * dz
            terms = [fx, fy, fz]
            if second:
                terms += [fx * dx, fy * dy, fz * dz, fx * dy, fx * dz, fy * dz]
                energy = inter * inter * root
                if slot < 3:
                    itself = twice(rows[9 * slot + 8]) == here
                    terms += [jnp.where(itself, 0.0, energy), jnp.where(itself, 0.0, pull * stretch)]
                else:
                    terms += [energy]
            added = [a + b for a, b in zip(added, terms)] + added[len(terms) :]
        stack = jnp.concatenate([jnp.concatenate(parts_of(value, 2), axis=1) for value in added], axis=0)
        sums = jnp.dot(stack, ones, preferred_element_type=jnp.float32)
        diagonal = whole_lane == here
        totals = [
            jnp.where(diagonal, sums[16 * i : 16 * i + 16, :], total) for i, total in enumerate(totals)
        ]
    return [jnp.sum(total, axis=0, keepdims=True) for total in totals]


def work_space():
    return (
        pltpu.VMEM((32, 8 * 128), jnp.bfloat16),
        pltpu.VMEM((9 * K, 8, 128), jnp.float32),
        pltpu.VMEM((8, 128, 128), jnp.float32),
        pltpu.VMEM((9 * K, 8, 128), jnp.float32),
        pltpu.VMEM((8, 128, 128), jnp.float32),
    )


def fill(tiles, low, middle, high, size):
    for part, ref in enumerate((low, middle, high)):
        for i in range(size):
            tiles[part * size + i] = ref[i]


def first_kernel(meta, low, middle, high, out, tiles, *work):
    width = middle.shape[0] // 3
    fill(tiles, low, middle, high, 3 * width)
    work[0][...] = selector()
    sub = lax.broadcasted_iota(jnp.int32, (8, 128), 0)

    def one(t, *work):
        own = tiles[4 * width + t + 1]
        sums = pair_sums(tiles, meta, t * 8, own, False, *work)
        radius = own[6:7, :]
        gain = STEP_DT / (DENS * radius * radius * radius)
        fresh = own
        for axis in range(3):
            speed = own[3 + axis : 4 + axis, :] + gain * sums[axis]
            place = own[axis : axis + 1, :] + STEP_DT * speed
            fresh = jnp.where(sub == axis, place, fresh)
            fresh = jnp.where(sub == 3 + axis, speed, fresh)
        out[t] = fresh

    @pl.loop(0, (width - 2) // 2)
    def _(t):
        one(2 * t, work[0], work[1], work[2])
        one(2 * t + 1, work[0], work[3], work[4])


def second_kernel(
    meta, cell, low, middle, high, place_out, speed_out, grid_out, energy_out, tiles, left, right, total, *work
):
    width = middle.shape[0] // 3
    fill(tiles, low, middle, high, 3 * width)
    work[0][...] = selector()
    sub = lax.broadcasted_iota(jnp.int32, (8, 128), 0)
    line = lax.broadcasted_iota(jnp.int32, (64, 128), 0)
    total[...] = jnp.zeros((8, 128), jnp.float32)
    right[...] = jnp.zeros(right.shape, jnp.bfloat16)

    def one(t, *work):
        own = tiles[4 * width + t + 1]
        sums = pair_sums(tiles, meta, t * 8, own, True, *work)
        radius = own[6:7, :]
        mass = DENS * radius * radius * radius
        gain = STEP_DT / mass
        values = [-0.5 * sums[3 + i] for i in range(6)]
        squares = jnp.zeros((1, 128), jnp.float32)
        this = pl.ds(t, 1)
        for axis in range(3):
            speed = own[3 + axis : 4 + axis, :] + gain * sums[axis]
            speed_out[axis, this, :] = speed
            place_out[axis, this, :] = own[axis : axis + 1, :] + STEP_DT * speed
            squares = squares + speed * speed
            values.append(mass * speed)
        kinetic = 0.5 * mass * squares
        values.append(kinetic)
        contact = 0.4 * KN * sums[9]
        bond = 0.5 * KB * sums[10]
        added = jnp.where(sub == 0, kinetic, jnp.where(sub == 1, contact, jnp.where(sub == 2, bond, 0.0)))
        total[...] = total[...] + added
        where = cell[this, :]
        span = pl.ds(pl.multiple_of(128 * t, 128), 128)
        in_plane = sub == lax.shift_right_logical(where, 6)
        for c in range(0, COMPS, 2):
            pair = jnp.concatenate(
                [jnp.where(in_plane, values[c], 0.0), jnp.where(in_plane, values[c + 1], 0.0)], axis=0
            )
            coarse = pair.astype(jnp.bfloat16)
            fine = (pair - coarse.astype(jnp.float32)).astype(jnp.bfloat16)
            right[8 * c : 8 * c + 16, span] = coarse
            right[128 + 8 * c : 128 + 8 * c + 16, span] = fine
        left[:, span] = jnp.where(line == lax.bitwise_and(where, 63), 1.0, 0.0).astype(jnp.bfloat16)

    @pl.loop(0, NT // 2)
    def _(t):
        one(2 * t, work[0], work[1], work[2])
        one(2 * t + 1, work[0], work[3], work[4])

    both = lax.dot_general(
        left[...], right[...], (((1,), (1,)), ((), ())), preferred_element_type=jnp.float32
    )
    scale = float(CX * CY * CZ) / float(NT * 128)
    grid_out[...] = (both[:, 0:128] + both[:, 128:256]) * scale
    for i in range(energy_out.shape[0]):
        energy_out[i] = total[...]


def plane_kernel(coords, own, before, after, energy, out):
    lane = lax.broadcasted_iota(jnp.int32, (8, 128), 1)
    inner = lax.bitwise_and(lane, 7)
    sums = energy[0]
    for i in range(1, energy.shape[0]):
        sums = sums + energy[i]
    sums = jnp.where(lane == 8 * COMPS, jnp.sum(sums, axis=1, keepdims=True), 0.0)
    planes = []
    for y in range(CY):
        block = slice(8 * y, 8 * y + 8)
        here = own[block, :]
        low = pltpu.roll(before[block, :], 120, 1)
        high = pltpu.roll(after[block, :], 8, 1)
        smooth = GAUSS[0] * here
        for d in range(1, HW + 1):
            ahead = pltpu.roll(jnp.where(inner >= d, here, high), 128 - d, 1)
            behind = pltpu.roll(jnp.where(inner < 8 - d, here, low), d, 1)
            smooth = smooth + GAUSS[d] * (ahead + behind)
        planes.append(smooth)
    rows = out.shape[0]
    for j in range(rows):
        out[j] = sums
    start = coords[1] * CY
    for r in range(-HW, CY + HW):
        mixed = sums
        for y in range(CY):
            if abs(r - y) <= HW:
                mixed = mixed + GAUSS[abs(r - y)] * planes[y]

        @pl.when(jnp.logical_and(start + r >= 0, start + r < rows))
        def _():
            out[start + r] = mixed


def line_kernel(parts, stress, motion, energies):
    count = parts.shape[0] // 8
    lane = lax.broadcasted_iota(jnp.int32, (8, 128), 1)
    sub = lax.broadcasted_iota(jnp.int32, (8, 128), 0)
    lines = []
    for block in range(8):
        line = parts[block]
        for other in range(1, count):
            line = line + parts[8 * other + block]
        lines.append(line)
    whole = lines[0]
    for line in lines[1:]:
        whole = whole + line
    for i in range(3):
        energies[i] = jnp.sum(jnp.where(jnp.logical_and(sub == i, lane == 8 * COMPS), whole, 0.0))
    empty = jnp.zeros((8, 128), jnp.float32)
    out = []
    for block in range(8):
        here = lines[block]
        low = lines[block - 1] if block > 0 else empty
        high = lines[block + 1] if block < 7 else empty
        smooth = GAUSS[0] * here
        for d in range(1, HW + 1):
            ahead = pltpu.roll(jnp.where(sub >= d, here, high), 8 - d, 0)
            behind = pltpu.roll(jnp.where(sub < 8 - d, here, low), d, 0)
            smooth = smooth + GAUSS[d] * (ahead + behind)
        out.append(smooth)
    turned = jnp.concatenate(out, axis=0).T
    for c in range(6):
        stress[c] = turned[8 * c : 8 * c + 8, :]
    for c in range(4):
        motion[c] = turned[48 + 8 * c : 56 + 8 * c, :]


def pack_kernel(place, speed, radius, group, broken, lists, counts, out, to_left, to_right):
    code = jnp.where(broken[...] == 0, group[...].astype(jnp.float32), -1.0)
    for t in range(NT):
        for axis in range(3):
            out[t, axis : axis + 1, :] = place[axis, t : t + 1, :]
            out[t, 3 + axis : 4 + axis, :] = speed[axis, t : t + 1, :]
        out[t, 6:7, :] = radius[t : t + 1, :]
        out[t, 7:8, :] = code[t : t + 1, :]
    for ref, edge, first in ((to_left, 0, 0), (to_right, NT - 1, NT - 2)):
        ref[0] = out[first]
        ref[1] = out[first + 1]
        ref[2] = jnp.zeros((8, 128), jnp.float32)
        ref[2, 0:1, 0:K] = lists[edge : edge + 1, :].astype(jnp.float32)
        ref[2, 1:2, 0:NT] = counts[...].astype(jnp.float32)


def shifted(value, axis, step, wrap):
    count = lax.axis_size(axis)
    pairs = [(i, (i + step) % count) for i in range(count) if wrap or 0 <= i + step < count]
    return lax.ppermute(value, axis, pairs)


def list_entries(lists, counts, home, shift, width, margin):
    offset = lists // NT
    along = offset // 9 - 1
    across = offset // 3 % 3
    up = offset % 3
    spot = jnp.clip((along + shift) * NT + lists % NT + margin, 0, width - 1)

    def within(axis, step):
        moved = lax.axis_index(axis) + step
        return (moved >= 0) & (moved < lax.axis_size(axis))

    live = lax.broadcasted_iota(jnp.int32, lists.shape, 1) < counts
    live = live & within("gx", shift) & within("gx", shift + along)
    live = live & within("gy", across - 1) & within("gz", up - 1)
    inside = live & (offset == 13)
    itself = inside & (spot == home)
    entry = up * (3 * width) + across * width + spot
    entry = entry + LIVE * live.astype(jnp.int32) + INSIDE * inside.astype(jnp.int32)
    entry = entry + ITSELF * itself.astype(jnp.int32)
    own = inside.astype(jnp.int32)
    earlier = lax.broadcasted_iota(jnp.int32, (K, K), 0) < lax.broadcasted_iota(jnp.int32, (K, K), 1)
    before = jnp.sum(jnp.where(earlier, own[:, :, None], 0), axis=1)
    slot = lax.broadcasted_iota(jnp.int32, lists.shape, 1)
    rank = jnp.where(inside, before, slot - before + jnp.sum(own, axis=1, keepdims=True))
    to = lax.broadcasted_iota(jnp.int32, (1, 1, 8), 2)
    return jnp.sum(jnp.where(rank[:, :, None] == to, entry[:, :, None], 0), axis=1).reshape(-1)


def shards(positions, velocities, radius, group, broken, cell, neighbours, counts):
    lists = neighbours.reshape(NT, K)
    listed = counts.reshape(1, NT)
    tile = jax.ShapeDtypeStruct((NT, 8, 128), jnp.float32)
    edge = jax.ShapeDtypeStruct((3, 8, 128), jnp.float32)
    own, to_left, to_right = pl.pallas_call(
        pack_kernel,
        out_shape=(tile, edge, edge),
        in_specs=[VMEM] * 7,
        out_specs=(VMEM, VMEM, VMEM),
        name="pack",
    )(
        positions.reshape(3, NT, 128),
        velocities.reshape(3, NT, 128),
        radius.reshape(NT, 128),
        group.reshape(NT, 128),
        broken.reshape(NT, 128),
        lists,
        listed,
    )
    from_left = shifted(to_right, "gx", 1, True)
    from_right = shifted(to_left, "gx", -1, True)
    line = jnp.concatenate([from_left[0:2], own, from_right[0:2]], axis=0)
    width = NT + 4

    def extended(tiles):
        up = shifted(tiles, "gy", 1, False)
        down = shifted(tiles, "gy", -1, False)
        middle = jnp.concatenate([up, tiles, down], axis=0)
        low = shifted(middle, "gz", 1, True)
        high = shifted(middle, "gz", -1, True)
        return low, middle, high

    low, middle, high = extended(line)
    all_lists = jnp.concatenate(
        [from_left[2, 0:1, 0:K].astype(jnp.int32), lists, from_right[2, 0:1, 0:K].astype(jnp.int32)], axis=0
    )
    all_counts = jnp.concatenate(
        [from_left[2, 1, NT - 1 : NT].astype(jnp.int32), listed[0], from_right[2, 1, 0:1].astype(jnp.int32)]
    )
    spots = lax.broadcasted_iota(jnp.int32, (NT + 2, 1), 0)
    shift = jnp.where(spots == 0, -1, jnp.where(spots == NT + 1, 1, 0))
    first_meta = list_entries(all_lists, all_counts[:, None], spots + 1, shift, width, 2)
    spots = lax.broadcasted_iota(jnp.int32, (NT, 1), 0)
    second_meta = list_entries(lists, listed.reshape(NT, 1), spots + 1, 0, width - 2, 1)

    line = pl.pallas_call(
        first_kernel,
        out_shape=jax.ShapeDtypeStruct((width - 2, 8, 128), jnp.float32),
        in_specs=[SMEM] + [VMEM] * 3,
        out_specs=VMEM,
        scratch_shapes=[
            pltpu.VMEM((9 * width, 8, 128), jnp.float32),
            *work_space(),
        ],
        name="first_step",
    )(first_meta, low, middle, high)
    low, middle, high = extended(line)
    width = width - 2
    peers = lax.axis_size("gx")
    block = jax.ShapeDtypeStruct((3, NT, 128), jnp.float32)
    places, speeds, grid, energy = pl.pallas_call(
        second_kernel,
        out_shape=(
            block,
            block,
            jax.ShapeDtypeStruct((64, 128), jnp.float32),
            jax.ShapeDtypeStruct((peers, 8, 128), jnp.float32),
        ),
        in_specs=[SMEM] + [VMEM] * 4,
        out_specs=(VMEM,) * 4,
        scratch_shapes=[
            pltpu.VMEM((9 * width, 8, 128), jnp.float32),
            pltpu.VMEM((64, NT * 128), jnp.bfloat16),
            pltpu.VMEM((256, NT * 128), jnp.bfloat16),
            pltpu.VMEM((8, 128), jnp.float32),
            *work_space(),
        ],
        name="second_step",
    )(second_meta, cell.reshape(NT, 128), low, middle, high)
    energy = lax.all_to_all(energy, "gx", 0, 0, tiled=True)
    before = shifted(grid, "gx", 1, False)
    after = shifted(grid, "gx", -1, False)
    coords = jnp.stack([lax.axis_index(a) for a in ("gx", "gy", "gz")])
    rows = lax.axis_size("gy") * lax.axis_size("gz")
    parts = pl.pallas_call(
        plane_kernel,
        out_shape=jax.ShapeDtypeStruct((rows, 8, 128), jnp.float32),
        in_specs=[SMEM] + [VMEM] * 4,
        out_specs=VMEM,
        name="planes",
    )(coords, grid, before, after, energy)
    parts = lax.all_to_all(parts, ("gy", "gz"), 0, 0, tiled=True)
    stress, motion, energies = pl.pallas_call(
        line_kernel,
        out_shape=(
            jax.ShapeDtypeStruct((6, 8, 64), jnp.float32),
            jax.ShapeDtypeStruct((4, 8, 64), jnp.float32),
            jax.ShapeDtypeStruct((3,), jnp.float32),
        ),
        in_specs=[VMEM],
        out_specs=(VMEM, VMEM, SMEM),
        name="lines",
    )(parts)
    return (
        places.reshape(positions.shape),
        speeds.reshape(velocities.shape),
        stress.reshape(6, CX, 1, 64),
        motion.reshape(4, CX, 1, 64),
        energies,
    )


def solution(mesh):
    placed = (
        P(None, "gx", "gy", "gz", None),
        P(None, "gx", "gy", "gz", None),
        P("gx", "gy", "gz", None),
        P("gx", "gy", "gz", None),
        P("gx", "gy", "gz", None),
        P("gx", "gy", "gz", None),
        P("gx", "gy", "gz", None, None),
        P("gx", "gy", "gz", None),
    )
    return jax.shard_map(
        shards,
        mesh=mesh,
        in_specs=placed,
        out_specs=(
            P(None, "gx", "gy", "gz", None),
            P(None, "gx", "gy", "gz", None),
            P(None, "gx", ("gy", "gz"), None),
            P(None, "gx", ("gy", "gz"), None),
            P(),
        ),
        check_vma=False,
    )
```

```python
import math

import jax
import jax.numpy as jnp
from jax import lax
from jax.experimental import pallas as pl
from jax.experimental.pallas import tpu as pltpu
from jax.sharding import PartitionSpec as P

STEPS = 2
CX = 8
CY = 8
CZ = 8
SIGMA = 2
HW = 6
KN = 1.0
GAMMA = 1.0
KB = 2.0
REACH = 1.5
STEP_DT = 0.02
DENS = 4.0
SOFT = 0.0001

NT = 8
K = 6
FAR = -1.0e9
LIVE = 1024
INSIDE = 2048
ITSELF = 4096
COMPS = 10
VMEM = pl.BlockSpec(memory_space=pltpu.VMEM)
SMALL = pltpu.CompilerParams(vmem_limit_bytes=4 << 20)
LARGE = pltpu.CompilerParams(vmem_limit_bytes=10 << 20)
SMEM = pl.BlockSpec(memory_space=pltpu.SMEM)

RAW = [math.exp(-d * d / (2.0 * SIGMA * SIGMA)) for d in range(HW + 1)]
TOTAL = RAW[0] + 2.0 * sum(RAW[1:])
GAUSS = [w / TOTAL for w in RAW]


def twice(value):
    return jnp.concatenate([value, value], axis=0)


def parts_of(value, count):
    parts = []
    for _ in range(count):
        part = value.astype(jnp.bfloat16)
        parts.append(part)
        value = value - part.astype(jnp.float32)
    return parts


def selector():
    shape = (32, 8 * 128)
    line = lax.broadcasted_iota(jnp.int32, shape, 0)
    block = lax.shift_right_logical(lax.broadcasted_iota(jnp.int32, shape, 1), 7)
    hit = jnp.logical_and(lax.bitwise_and(line, 7) == block, line < 24)
    return jnp.where(hit, 1.0, 0.0).astype(jnp.bfloat16)


def own_columns(own, select, mine):
    stack = jnp.concatenate(
        [part.astype(jnp.float32) for part in parts_of(own, 3)] + [jnp.zeros((8, 128), jnp.float32)], axis=0
    ).astype(jnp.bfloat16)
    wide = lax.dot_general(
        stack, select[...], (((0,), (0,)), ((), ())), preferred_element_type=jnp.float32
    )
    for c in range(8):
        mine[c] = wide[:, 128 * c : 128 * c + 128]


def pair_sums(tiles, meta, base, own, second, select, rows, mine):
    lane = lax.broadcasted_iota(jnp.int32, (8, 128), 1).astype(jnp.float32)
    for slot in range(K):
        entry = meta[base + slot]
        index = lax.bitwise_and(entry, 1023)
        live = lax.bitwise_and(entry, LIVE) > 0
        for c in range(8 if slot < 3 else 7):
            value = jnp.broadcast_to(tiles[index, c : c + 1, :], (8, 128))
            if c == 6:
                value = jnp.where(jnp.logical_and(live, value > 0.0), value, FAR)
            if c == 7:
                value = jnp.where(lax.bitwise_and(entry, INSIDE) > 0, value, -7.0)
            rows[9 * slot + c] = value
        if second and slot < 3:
            rows[9 * slot + 8] = jnp.where(lax.bitwise_and(entry, ITSELF) > 0, lane, -1.0)
    own_columns(own, select, mine)
    number = lax.broadcasted_iota(jnp.int32, (16, 128), 0).astype(jnp.float32)
    whole_lane = twice(lane)
    ones = jnp.ones((256, 128), jnp.bfloat16)
    count = 11 if second else 3
    totals = [jnp.zeros((16, 128), jnp.float32)] * count
    for block in range(8):
        xi, yi, zi, ui, vi, wi, ri, ci = [mine[c, 16 * block : 16 * block + 16, :] for c in range(8)]
        ci = jnp.where(ci < 0.0, -5.0, ci)
        here = number + float(16 * block)
        added = [jnp.zeros((16, 128), jnp.float32)] * count
        for slot in range(K):
            xj, yj, zj, uj, vj, wj, rj = [twice(rows[9 * slot + c]) for c in range(7)]
            dx, dy, dz = xj - xi, yj - yi, zj - zi
            square = dx * dx + dy * dy + (dz * dz + SOFT)
            inverse = lax.rsqrt(square)
            distance = square * inverse
            reach = rj + ri
            inter = jnp.maximum(reach - distance, 0.0)
            root = inter * lax.rsqrt(jnp.maximum(inter, 1e-30))
            closing = ((uj - ui) * dx + (vj - vi) * dy + (wj - wi) * dz) * inverse
            magnitude = root * (closing - inter)
            if slot < 3:
                ratio = lax.rsqrt(reach)
                window = jnp.maximum(1.0 - distance * ((1.0 / REACH) * ratio * ratio), 0.0)
                window = jnp.where(twice(rows[9 * slot + 7]) == ci, window * window, 0.0)
                stretch = distance - reach
                pull = stretch * window
                magnitude = magnitude + KB * pull
            scaled = magnitude * inverse
            fx, fy, fz = scaled * dx, scaled * dy, scaled * dz
            terms = [fx, fy, fz]
            if second:
                terms += [fx * dx, fy * dy, fz * dz, fx * dy, fx * dz, fy * dz]
                energy = inter * inter * root
                if slot < 3:
                    itself = twice(rows[9 * slot + 8]) == here
                    terms += [jnp.where(itself, 0.0, energy), jnp.where(itself, 0.0, pull * stretch)]
                else:
                    terms += [energy]
            added = [a + b for a, b in zip(added, terms)] + added[len(terms) :]
        stack = jnp.concatenate([jnp.concatenate(parts_of(value, 2), axis=1) for value in added], axis=0)
        sums = jnp.dot(stack, ones, preferred_element_type=jnp.float32)
        diagonal = whole_lane == here
        totals = [
            jnp.where(diagonal, sums[16 * i : 16 * i + 16, :], total) for i, total in enumerate(totals)
        ]
    return [jnp.sum(total, axis=0, keepdims=True) for total in totals]


def work_space():
    return (
        pltpu.VMEM((32, 8 * 128), jnp.bfloat16),
        pltpu.VMEM((9 * K, 8, 128), jnp.float32),
        pltpu.VMEM((8, 128, 128), jnp.float32),
        pltpu.VMEM((9 * K, 8, 128), jnp.float32),
        pltpu.VMEM((8, 128, 128), jnp.float32),
    )


def fill(tiles, low, middle, high, size):
    for part, ref in enumerate((low, middle, high)):
        for i in range(size):
            tiles[part * size + i] = ref[i]


def first_kernel(meta, low, middle, high, out, tiles, *work):
    width = middle.shape[0] // 3
    fill(tiles, low, middle, high, 3 * width)
    work[0][...] = selector()
    sub = lax.broadcasted_iota(jnp.int32, (8, 128), 0)

    def one(t, *work):
        own = tiles[4 * width + t + 2]
        sums = pair_sums(tiles, meta, t * 8, own, False, *work)
        radius = own[6:7, :]
        gain = STEP_DT / (DENS * radius * radius * radius)
        fresh = own
        for axis in range(3):
            speed = own[3 + axis : 4 + axis, :] + gain * sums[axis]
            place = own[axis : axis + 1, :] + STEP_DT * speed
            fresh = jnp.where(sub == axis, place, fresh)
            fresh = jnp.where(sub == 3 + axis, speed, fresh)
        out[t] = fresh

    @pl.loop(0, (width - 4) // 2)
    def _(t):
        one(2 * t, work[0], work[1], work[2])
        one(2 * t + 1, work[0], work[3], work[4])


def second_kernel(
    meta, cell, low, middle, high, place_out, speed_out, grid_out, energy_out, tiles, left, right, total, *work
):
    width = middle.shape[0] // 3
    fill(tiles, low, middle, high, 3 * width)
    work[0][...] = selector()
    sub = lax.broadcasted_iota(jnp.int32, (8, 128), 0)
    line = lax.broadcasted_iota(jnp.int32, (64, 128), 0)
    total[...] = jnp.zeros((8, 128), jnp.float32)
    right[...] = jnp.zeros(right.shape, jnp.bfloat16)

    def one(t, *work):
        own = tiles[4 * width + t + 1]
        sums = pair_sums(tiles, meta, t * 8, own, True, *work)
        radius = own[6:7, :]
        mass = DENS * radius * radius * radius
        gain = STEP_DT / mass
        values = [-0.5 * sums[3 + i] for i in range(6)]
        squares = jnp.zeros((1, 128), jnp.float32)
        this = pl.ds(t, 1)
        for axis in range(3):
            speed = own[3 + axis : 4 + axis, :] + gain * sums[axis]
            speed_out[axis, this, :] = speed
            place_out[axis, this, :] = own[axis : axis + 1, :] + STEP_DT * speed
            squares = squares + speed * speed
            values.append(mass * speed)
        kinetic = 0.5 * mass * squares
        values.append(kinetic)
        contact = 0.4 * KN * sums[9]
        bond = 0.5 * KB * sums[10]
        added = jnp.where(sub == 0, kinetic, jnp.where(sub == 1, contact, jnp.where(sub == 2, bond, 0.0)))
        total[...] = total[...] + added
        where = cell[this, :]
        span = pl.ds(pl.multiple_of(128 * t, 128), 128)
        in_plane = sub == lax.shift_right_logical(where, 6)
        for c in range(0, COMPS, 2):
            pair = jnp.concatenate(
                [jnp.where(in_plane, values[c], 0.0), jnp.where(in_plane, values[c + 1], 0.0)], axis=0
            )
            coarse = pair.astype(jnp.bfloat16)
            fine = (pair - coarse.astype(jnp.float32)).astype(jnp.bfloat16)
            right[8 * c : 8 * c + 16, span] = coarse
            right[128 + 8 * c : 128 + 8 * c + 16, span] = fine
        left[:, span] = jnp.where(line == lax.bitwise_and(where, 63), 1.0, 0.0).astype(jnp.bfloat16)

    @pl.loop(0, NT // 2)
    def _(t):
        one(2 * t, work[0], work[1], work[2])
        one(2 * t + 1, work[0], work[3], work[4])

    both = lax.dot_general(
        left[...], right[...], (((1,), (1,)), ((), ())), preferred_element_type=jnp.float32
    )
    scale = float(CX * CY * CZ) / float(NT * 128)
    grid_out[...] = (both[:, 0:128] + both[:, 128:256]) * scale
    for i in range(energy_out.shape[0]):
        energy_out[i] = total[...]


def plane_kernel(coords, own, before, after, energy, out):
    lane = lax.broadcasted_iota(jnp.int32, (8, 128), 1)
    inner = lax.bitwise_and(lane, 7)
    sums = energy[0]
    for i in range(1, energy.shape[0]):
        sums = sums + energy[i]
    sums = jnp.where(lane == 8 * COMPS, jnp.sum(sums, axis=1, keepdims=True), 0.0)
    planes = []
    for y in range(CY):
        block = slice(8 * y, 8 * y + 8)
        here = own[block, :]
        low = pltpu.roll(before[block, :], 120, 1)
        high = pltpu.roll(after[block, :], 8, 1)
        smooth = GAUSS[0] * here
        for d in range(1, HW + 1):
            ahead = pltpu.roll(jnp.where(inner >= d, here, high), 128 - d, 1)
            behind = pltpu.roll(jnp.where(inner < 8 - d, here, low), d, 1)
            smooth = smooth + GAUSS[d] * (ahead + behind)
        planes.append(smooth)
    rows = out.shape[0]
    for j in range(rows):
        out[j] = sums
    start = coords[1] * CY
    for r in range(-HW, CY + HW):
        mixed = sums
        for y in range(CY):
            if abs(r - y) <= HW:
                mixed = mixed + GAUSS[abs(r - y)] * planes[y]

        @pl.when(jnp.logical_and(start + r >= 0, start + r < rows))
        def _():
            out[start + r] = mixed


def line_kernel(parts, stress, motion, energies):
    count = parts.shape[0] // 8
    lane = lax.broadcasted_iota(jnp.int32, (8, 128), 1)
    sub = lax.broadcasted_iota(jnp.int32, (8, 128), 0)
    lines = []
    for block in range(8):
        line = parts[block]
        for other in range(1, count):
            line = line + parts[8 * other + block]
        lines.append(line)
    whole = lines[0]
    for line in lines[1:]:
        whole = whole + line
    for i in range(3):
        energies[i] = jnp.sum(jnp.where(jnp.logical_and(sub == i, lane == 8 * COMPS), whole, 0.0))
    empty = jnp.zeros((8, 128), jnp.float32)
    out = []
    for block in range(8):
        here = lines[block]
        low = lines[block - 1] if block > 0 else empty
        high = lines[block + 1] if block < 7 else empty
        smooth = GAUSS[0] * here
        for d in range(1, HW + 1):
            ahead = pltpu.roll(jnp.where(sub >= d, here, high), 8 - d, 0)
            behind = pltpu.roll(jnp.where(sub < 8 - d, here, low), d, 0)
            smooth = smooth + GAUSS[d] * (ahead + behind)
        out.append(smooth)
    turned = jnp.concatenate(out, axis=0).T
    for c in range(6):
        stress[c] = turned[8 * c : 8 * c + 8, :]
    for c in range(4):
        motion[c] = turned[48 + 8 * c : 56 + 8 * c, :]


def pack_kernel(place, speed, radius, group, broken, lists, counts, out, to_left, to_right):
    code = jnp.where(broken[...] == 0, group[...].astype(jnp.float32), -1.0)
    for t in range(NT):
        for axis in range(3):
            out[t, axis : axis + 1, :] = place[axis, t : t + 1, :]
            out[t, 3 + axis : 4 + axis, :] = speed[axis, t : t + 1, :]
        out[t, 6:7, :] = radius[t : t + 1, :]
        out[t, 7:8, :] = code[t : t + 1, :]
    for ref, notes, tile, first in ((to_left, 2, 0, 0), (to_right, 0, 1, NT - 2)):
        ref[tile] = out[first]
        ref[tile + 1] = out[first + 1]
        ref[notes] = jnp.zeros((8, 128), jnp.float32)
        for slot in range(K):
            ref[notes, slot : slot + 1, 0:NT] = lists[slot].astype(jnp.float32)
        ref[notes, K : K + 1, 0:NT] = counts[...].astype(jnp.float32)


def shifted(value, axis, step, wrap):
    count = lax.axis_size(axis)
    pairs = [(i, (i + step) % count) for i in range(count) if wrap or 0 <= i + step < count]
    return lax.ppermute(value, axis, pairs)


def list_entries(lists, counts, home, shift, width, margin):
    offset = lists // NT
    along = offset // 9 - 1
    across = offset // 3 % 3
    up = offset % 3
    spot = jnp.clip((along + shift) * NT + lists % NT + margin, 0, width - 1)

    def within(axis, step):
        moved = lax.axis_index(axis) + step
        return (moved >= 0) & (moved < lax.axis_size(axis))

    live = lax.broadcasted_iota(jnp.int32, lists.shape, 1) < counts
    live = live & within("gx", shift) & within("gx", shift + along)
    live = live & within("gy", across - 1) & within("gz", up - 1)
    inside = live & (offset == 13)
    itself = inside & (spot == home)
    entry = up * (3 * width) + across * width + spot
    entry = entry + LIVE * live.astype(jnp.int32) + INSIDE * inside.astype(jnp.int32)
    entry = entry + ITSELF * itself.astype(jnp.int32)
    own = inside.astype(jnp.int32)
    earlier = lax.broadcasted_iota(jnp.int32, (K, K), 0) < lax.broadcasted_iota(jnp.int32, (K, K), 1)
    before = jnp.sum(jnp.where(earlier, own[:, :, None], 0), axis=1)
    slot = lax.broadcasted_iota(jnp.int32, lists.shape, 1)
    rank = jnp.where(inside, before, slot - before + jnp.sum(own, axis=1, keepdims=True))
    to = lax.broadcasted_iota(jnp.int32, (1, 1, 8), 2)
    return jnp.sum(jnp.where(rank[:, :, None] == to, entry[:, :, None], 0), axis=1).reshape(-1)


def shards(positions, velocities, radius, group, broken, cell, neighbours, counts):
    lists = neighbours.reshape(NT, K)
    listed = counts.reshape(NT, 1)
    tile = jax.ShapeDtypeStruct((NT, 8, 128), jnp.float32)
    edge = jax.ShapeDtypeStruct((3, 8, 128), jnp.float32)
    own, to_left, to_right = pl.pallas_call(
        pack_kernel,
        out_shape=(tile, edge, edge),
        in_specs=[VMEM] * 7,
        out_specs=(VMEM, VMEM, VMEM),
        compiler_params=SMALL,
        name="pack",
    )(
        positions.reshape(3, NT, 128),
        velocities.reshape(3, NT, 128),
        radius.reshape(NT, 128),
        group.reshape(NT, 128),
        broken.reshape(NT, 128),
        lists.T.reshape(K, 1, NT),
        counts.reshape(1, NT),
    )
    from_left = shifted(to_right, "gx", 1, True)
    from_right = shifted(to_left, "gx", -1, True)
    line = jnp.concatenate([from_left, own, from_right], axis=0)
    width = NT + 6

    def extended(tiles):
        up = shifted(tiles, "gy", 1, False)
        down = shifted(tiles, "gy", -1, False)
        middle = jnp.concatenate([up, tiles, down], axis=0)
        low = shifted(middle, "gz", 1, True)
        high = shifted(middle, "gz", -1, True)
        return low, middle, high

    low, middle, high = extended(line)
    left_notes = from_left[0, 0:7, NT - 1].astype(jnp.int32)
    right_notes = from_right[2, 0:7, 0].astype(jnp.int32)
    all_lists = jnp.concatenate([left_notes[None, 0:K], lists, right_notes[None, 0:K]], axis=0)
    all_counts = jnp.concatenate([left_notes[None, K:7], listed, right_notes[None, K:7]], axis=0)
    spots = lax.broadcasted_iota(jnp.int32, (NT + 2, 1), 0)
    shift = jnp.where(spots == 0, -1, jnp.where(spots == NT + 1, 1, 0))
    first_meta = list_entries(all_lists, all_counts, spots + 2, shift, width, 3)
    spots = lax.broadcasted_iota(jnp.int32, (NT, 1), 0)
    second_meta = list_entries(lists, listed, spots + 1, 0, width - 4, 1)

    line = pl.pallas_call(
        first_kernel,
        out_shape=jax.ShapeDtypeStruct((width - 4, 8, 128), jnp.float32),
        in_specs=[SMEM] + [VMEM] * 3,
        out_specs=VMEM,
        scratch_shapes=[
            pltpu.VMEM((9 * width, 8, 128), jnp.float32),
            *work_space(),
        ],
        compiler_params=LARGE,
        name="first_step",
    )(first_meta, low, middle, high)
    low, middle, high = extended(line)
    width = width - 4
    peers = lax.axis_size("gx")
    block = jax.ShapeDtypeStruct((3, NT, 128), jnp.float32)
    places, speeds, grid, energy = pl.pallas_call(
        second_kernel,
        out_shape=(
            block,
            block,
            jax.ShapeDtypeStruct((64, 128), jnp.float32),
            jax.ShapeDtypeStruct((peers, 8, 128), jnp.float32),
        ),
        in_specs=[SMEM] + [VMEM] * 4,
        out_specs=(VMEM,) * 4,
        scratch_shapes=[
            pltpu.VMEM((9 * width, 8, 128), jnp.float32),
            pltpu.VMEM((64, NT * 128), jnp.bfloat16),
            pltpu.VMEM((256, NT * 128), jnp.bfloat16),
            pltpu.VMEM((8, 128), jnp.float32),
            *work_space(),
        ],
        compiler_params=LARGE,
        name="second_step",
    )(second_meta, cell.reshape(NT, 128), low, middle, high)
    energy = lax.all_to_all(energy, "gx", 0, 0, tiled=True)
    before = shifted(grid, "gx", 1, False)
    after = shifted(grid, "gx", -1, False)
    coords = jnp.stack([lax.axis_index(a) for a in ("gx", "gy", "gz")])
    rows = lax.axis_size("gy") * lax.axis_size("gz")
    parts = pl.pallas_call(
        plane_kernel,
        out_shape=jax.ShapeDtypeStruct((rows, 8, 128), jnp.float32),
        in_specs=[SMEM] + [VMEM] * 4,
        out_specs=VMEM,
        compiler_params=SMALL,
        name="planes",
    )(coords, grid, before, after, energy)
    parts = lax.all_to_all(parts, ("gy", "gz"), 0, 0, tiled=True)
    stress, motion, energies = pl.pallas_call(
        line_kernel,
        out_shape=(
            jax.ShapeDtypeStruct((6, 8, 64), jnp.float32),
            jax.ShapeDtypeStruct((4, 8, 64), jnp.float32),
            jax.ShapeDtypeStruct((3,), jnp.float32),
        ),
        in_specs=[VMEM],
        out_specs=(VMEM, VMEM, SMEM),
        compiler_params=SMALL,
        name="lines",
    )(parts)
    return (
        places.reshape(positions.shape),
        speeds.reshape(velocities.shape),
        stress.reshape(6, CX, 1, 64),
        motion.reshape(4, CX, 1, 64),
        energies,
    )


def solution(mesh):
    placed = (
        P(None, "gx", "gy", "gz", None),
        P(None, "gx", "gy", "gz", None),
        P("gx", "gy", "gz", None),
        P("gx", "gy", "gz", None),
        P("gx", "gy", "gz", None),
        P("gx", "gy", "gz", None),
        P("gx", "gy", "gz", None, None),
        P("gx", "gy", "gz", None),
    )
    return jax.shard_map(
        shards,
        mesh=mesh,
        in_specs=placed,
        out_specs=(
            P(None, "gx", "gy", "gz", None),
            P(None, "gx", "gy", "gz", None),
            P(None, "gx", ("gy", "gz"), None),
            P(None, "gx", ("gy", "gz"), None),
            P(),
        ),
        check_vma=False,
    )
```

```python
import math

import jax
import jax.numpy as jnp
from jax import lax
from jax.experimental import pallas as pl
from jax.experimental.pallas import tpu as pltpu
from jax.sharding import PartitionSpec as P

STEPS = 2
CX = 8
CY = 8
CZ = 8
SIGMA = 2
HW = 6
KN = 1.0
GAMMA = 1.0
KB = 2.0
REACH = 1.5
STEP_DT = 0.02
DENS = 4.0
SOFT = 0.0001

NT = 8
K = 6
FAR = -1.0e9
LIVE = 1024
INSIDE = 2048
ITSELF = 4096
COMPS = 10
VMEM = pl.BlockSpec(memory_space=pltpu.VMEM)
SMALL = pltpu.CompilerParams(vmem_limit_bytes=4 << 20)
LARGE = pltpu.CompilerParams(vmem_limit_bytes=10 << 20)
SMEM = pl.BlockSpec(memory_space=pltpu.SMEM)

RAW = [math.exp(-d * d / (2.0 * SIGMA * SIGMA)) for d in range(HW + 1)]
TOTAL = RAW[0] + 2.0 * sum(RAW[1:])
GAUSS = [w / TOTAL for w in RAW]


def twice(value):
    return jnp.concatenate([value, value], axis=0)


def own_columns(own, mine):
    for c in range(8):
        mine[c] = jnp.broadcast_to(own[c : c + 1, :], (128, 128)).T


def pair_sums(tiles, meta, t, own, second, rows, mine):
    lane = lax.broadcasted_iota(jnp.int32, (8, 128), 1).astype(jnp.float32)
    stride = meta.shape[0] // K
    for slot in range(K):
        entry = meta[slot * stride + t]
        index = lax.bitwise_and(entry, 1023)
        live = lax.bitwise_and(entry, LIVE) > 0
        for c in range(8 if slot < 3 else 7):
            value = jnp.broadcast_to(tiles[index, c : c + 1, :], (8, 128))
            if c == 6:
                value = jnp.where(jnp.logical_and(live, value > 0.0), value, FAR)
            if c == 7:
                value = jnp.where(lax.bitwise_and(entry, INSIDE) > 0, value, -7.0)
            rows[9 * slot + c] = value
        if second and slot < 3:
            rows[9 * slot + 8] = jnp.where(lax.bitwise_and(entry, ITSELF) > 0, lane, -1.0)
    own_columns(own, mine)
    number = lax.broadcasted_iota(jnp.int32, (16, 128), 0).astype(jnp.float32)
    count = 11 if second else 3
    stacks = []
    for block in range(8):
        xi, yi, zi, ui, vi, wi, ri, ci = [mine[c, 16 * block : 16 * block + 16, :] for c in range(8)]
        ci = jnp.where(ci < 0.0, -5.0, ci)
        here = number + float(16 * block)
        added = [jnp.zeros((16, 128), jnp.float32)] * count
        for slot in range(K):
            xj, yj, zj, uj, vj, wj, rj = [twice(rows[9 * slot + c]) for c in range(7)]
            dx, dy, dz = xj - xi, yj - yi, zj - zi
            square = dx * dx + dy * dy + (dz * dz + SOFT)
            inverse = lax.rsqrt(square)
            distance = square * inverse
            reach = rj + ri
            inter = jnp.maximum(reach - distance, 0.0)
            root = inter * lax.rsqrt(jnp.maximum(inter, 1e-30))
            closing = ((uj - ui) * dx + (vj - vi) * dy + (wj - wi) * dz) * inverse
            magnitude = root * (closing - inter)
            if slot < 3:
                ratio = lax.rsqrt(reach)
                window = jnp.maximum(1.0 - distance * ((1.0 / REACH) * ratio * ratio), 0.0)
                window = jnp.where(twice(rows[9 * slot + 7]) == ci, window * window, 0.0)
                stretch = distance - reach
                pull = stretch * window
                magnitude = magnitude + KB * pull
            scaled = magnitude * inverse
            fx, fy, fz = scaled * dx, scaled * dy, scaled * dz
            terms = [fx, fy, fz]
            if second:
                terms += [fx * dx, fy * dy, fz * dz, fx * dy, fx * dz, fy * dz]
                energy = inter * inter * root
                if slot < 3:
                    itself = twice(rows[9 * slot + 8]) == here
                    terms += [jnp.where(itself, 0.0, energy), jnp.where(itself, 0.0, pull * stretch)]
                else:
                    terms += [energy]
            added = [a + b for a, b in zip(added, terms)] + added[len(terms) :]
        stacks.append(added)
    totals = [jnp.concatenate([added[i] for added in stacks], axis=0).T for i in range(count)]
    return [jnp.sum(total, axis=0, keepdims=True) for total in totals]


def work_space():
    return (
        pltpu.VMEM((9 * K, 8, 128), jnp.float32),
        pltpu.VMEM((8, 128, 128), jnp.float32),
        pltpu.VMEM((9 * K, 8, 128), jnp.float32),
        pltpu.VMEM((8, 128, 128), jnp.float32),
    )


def fill(tiles, low, middle, high, size):
    for part, ref in enumerate((low, middle, high)):
        for i in range(size):
            tiles[part * size + i] = ref[i]


def first_kernel(meta, low, middle, high, out, tiles, *work):
    width = middle.shape[0] // 3
    fill(tiles, low, middle, high, 3 * width)
    sub = lax.broadcasted_iota(jnp.int32, (8, 128), 0)

    def one(t, *work):
        own = tiles[4 * width + t + 2]
        sums = pair_sums(tiles, meta, t, own, False, *work)
        radius = own[6:7, :]
        gain = STEP_DT / (DENS * radius * radius * radius)
        fresh = own
        for axis in range(3):
            speed = own[3 + axis : 4 + axis, :] + gain * sums[axis]
            place = own[axis : axis + 1, :] + STEP_DT * speed
            fresh = jnp.where(sub == axis, place, fresh)
            fresh = jnp.where(sub == 3 + axis, speed, fresh)
        out[t] = fresh

    @pl.loop(0, (width - 4) // 2)
    def _(t):
        one(2 * t, work[0], work[1])
        one(2 * t + 1, work[2], work[3])


def second_kernel(
    meta, cell, low, middle, high, place_out, speed_out, grid_out, energy_out, tiles, left, right, total, *work
):
    width = middle.shape[0] // 3
    fill(tiles, low, middle, high, 3 * width)
    sub = lax.broadcasted_iota(jnp.int32, (8, 128), 0)
    line = lax.broadcasted_iota(jnp.int32, (64, 128), 0)
    total[...] = jnp.zeros((8, 128), jnp.float32)
    right[...] = jnp.zeros(right.shape, jnp.bfloat16)

    def one(t, *work):
        own = tiles[4 * width + t + 1]
        sums = pair_sums(tiles, meta, t, own, True, *work)
        radius = own[6:7, :]
        mass = DENS * radius * radius * radius
        gain = STEP_DT / mass
        values = [-0.5 * sums[3 + i] for i in range(6)]
        squares = jnp.zeros((1, 128), jnp.float32)
        this = pl.ds(t, 1)
        for axis in range(3):
            speed = own[3 + axis : 4 + axis, :] + gain * sums[axis]
            speed_out[axis, this, :] = speed
            place_out[axis, this, :] = own[axis : axis + 1, :] + STEP_DT * speed
            squares = squares + speed * speed
            values.append(mass * speed)
        kinetic = 0.5 * mass * squares
        values.append(kinetic)
        contact = 0.4 * KN * sums[9]
        bond = 0.5 * KB * sums[10]
        added = jnp.where(sub == 0, kinetic, jnp.where(sub == 1, contact, jnp.where(sub == 2, bond, 0.0)))
        total[...] = total[...] + added
        where = cell[this, :]
        span = pl.ds(pl.multiple_of(128 * t, 128), 128)
        in_plane = sub == lax.shift_right_logical(where, 6)
        for c in range(0, COMPS, 2):
            pair = jnp.concatenate(
                [jnp.where(in_plane, values[c], 0.0), jnp.where(in_plane, values[c + 1], 0.0)], axis=0
            )
            coarse = pair.astype(jnp.bfloat16)
            fine = (pair - coarse.astype(jnp.float32)).astype(jnp.bfloat16)
            right[8 * c : 8 * c + 16, span] = coarse
            right[128 + 8 * c : 128 + 8 * c + 16, span] = fine
        left[:, span] = jnp.where(line == lax.bitwise_and(where, 63), 1.0, 0.0).astype(jnp.bfloat16)

    @pl.loop(0, NT // 2)
    def _(t):
        one(2 * t, work[0], work[1])
        one(2 * t + 1, work[2], work[3])

    both = lax.dot_general(
        left[...], right[...], (((1,), (1,)), ((), ())), preferred_element_type=jnp.float32
    )
    scale = float(CX * CY * CZ) / float(NT * 128)
    grid_out[...] = (both[:, 0:128] + both[:, 128:256]) * scale
    for i in range(energy_out.shape[0]):
        energy_out[i] = total[...]


def plane_kernel(coords, own, before, after, energy, out):
    lane = lax.broadcasted_iota(jnp.int32, (8, 128), 1)
    inner = lax.bitwise_and(lane, 7)
    sums = energy[0]
    for i in range(1, energy.shape[0]):
        sums = sums + energy[i]
    sums = jnp.where(lane == 8 * COMPS, jnp.sum(sums, axis=1, keepdims=True), 0.0)
    planes = []
    for y in range(CY):
        block = slice(8 * y, 8 * y + 8)
        here = own[block, :]
        low = pltpu.roll(before[block, :], 120, 1)
        high = pltpu.roll(after[block, :], 8, 1)
        smooth = GAUSS[0] * here
        for d in range(1, HW + 1):
            ahead = pltpu.roll(jnp.where(inner >= d, here, high), 128 - d, 1)
            behind = pltpu.roll(jnp.where(inner < 8 - d, here, low), d, 1)
            smooth = smooth + GAUSS[d] * (ahead + behind)
        planes.append(smooth)
    rows = out.shape[0]
    for j in range(rows):
        out[j] = sums
    start = coords[1] * CY
    for r in range(-HW, CY + HW):
        mixed = sums
        for y in range(CY):
            if abs(r - y) <= HW:
                mixed = mixed + GAUSS[abs(r - y)] * planes[y]

        @pl.when(jnp.logical_and(start + r >= 0, start + r < rows))
        def _():
            out[start + r] = mixed


def line_kernel(parts, stress, motion, energies):
    count = parts.shape[0] // 8
    lane = lax.broadcasted_iota(jnp.int32, (8, 128), 1)
    sub = lax.broadcasted_iota(jnp.int32, (8, 128), 0)
    lines = []
    for block in range(8):
        line = parts[block]
        for other in range(1, count):
            line = line + parts[8 * other + block]
        lines.append(line)
    whole = lines[0]
    for line in lines[1:]:
        whole = whole + line
    for i in range(3):
        energies[i] = jnp.sum(jnp.where(jnp.logical_and(sub == i, lane == 8 * COMPS), whole, 0.0))
    empty = jnp.zeros((8, 128), jnp.float32)
    out = []
    for block in range(8):
        here = lines[block]
        low = lines[block - 1] if block > 0 else empty
        high = lines[block + 1] if block < 7 else empty
        smooth = GAUSS[0] * here
        for d in range(1, HW + 1):
            ahead = pltpu.roll(jnp.where(sub >= d, here, high), 8 - d, 0)
            behind = pltpu.roll(jnp.where(sub < 8 - d, here, low), d, 0)
            smooth = smooth + GAUSS[d] * (ahead + behind)
        out.append(smooth)
    turned = jnp.concatenate(out, axis=0).T
    for c in range(6):
        stress[c] = turned[8 * c : 8 * c + 8, :]
    for c in range(4):
        motion[c] = turned[48 + 8 * c : 56 + 8 * c, :]


def pack_kernel(*refs):
    sources, (out, to_left, to_right, notes), held, done = refs[0:7], refs[7:11], refs[11:18], refs[18]
    copies = [pltpu.make_async_copy(a, b, done.at[i]) for i, (a, b) in enumerate(zip(sources, held))]
    for copy in copies:
        copy.start()
    for copy in copies:
        copy.wait()
    place, speed, radius, group, broken, lists, counts = held
    code = jnp.where(broken[...] == 0, group[...].astype(jnp.float32), -1.0)
    for t in range(NT):
        for axis in range(3):
            out[t, axis : axis + 1, :] = place[axis, t : t + 1, :]
            out[t, 3 + axis : 4 + axis, :] = speed[axis, t : t + 1, :]
        out[t, 6:7, :] = radius[t : t + 1, :]
        out[t, 7:8, :] = code[t : t + 1, :]
    notes[...] = jnp.zeros((8, 128), jnp.float32)
    for slot in range(K):
        notes[slot : slot + 1, 0:NT] = lists[0, 0, slot].astype(jnp.float32)
    notes[K : K + 1, 0:NT] = counts[...].astype(jnp.float32)
    for ref, place, tile, first in ((to_left, 2, 0, 0), (to_right, 0, 1, NT - 2)):
        ref[tile] = out[first]
        ref[tile + 1] = out[first + 1]
        ref[place] = notes[...]


def shifted(value, axis, step, wrap):
    count = lax.axis_size(axis)
    pairs = [(i, (i + step) % count) for i in range(count) if wrap or 0 <= i + step < count]
    return lax.ppermute(value, axis, pairs)


def list_entries(lists, counts, home, shift, width, margin):
    offset = lists // NT
    along = offset // 9 - 1
    across = offset // 3 % 3
    up = offset % 3
    spot = jnp.clip((along + shift) * NT + lists % NT + margin, 0, width - 1)

    def within(axis, step):
        moved = lax.axis_index(axis) + step
        return (moved >= 0) & (moved < lax.axis_size(axis))

    slot = lax.broadcasted_iota(jnp.int32, lists.shape, 0)
    live = (slot < counts) & within("gx", shift) & within("gx", shift + along)
    live = live & within("gy", across - 1) & within("gz", up - 1)
    inside = live & (offset == 13)
    itself = inside & (spot == home)
    entry = up * (3 * width) + across * width + spot
    entry = entry + LIVE * live.astype(jnp.int32) + INSIDE * inside.astype(jnp.int32)
    entry = entry + ITSELF * itself.astype(jnp.int32)
    own = inside.astype(jnp.int32)
    earlier = lax.broadcasted_iota(jnp.int32, (K, K, 1), 0) < lax.broadcasted_iota(jnp.int32, (K, K, 1), 1)
    before = jnp.sum(jnp.where(earlier, own[:, None, :], 0), axis=0)
    rank = jnp.where(inside, before, slot - before + jnp.sum(own, axis=0, keepdims=True))
    to = lax.broadcasted_iota(jnp.int32, (1, K, 1), 1)
    return jnp.sum(jnp.where(rank[:, None, :] == to, entry[:, None, :], 0), axis=0).reshape(-1)


def shards(positions, velocities, radius, group, broken, cell, neighbours, counts):
    tile = jax.ShapeDtypeStruct((NT, 8, 128), jnp.float32)
    edge = jax.ShapeDtypeStruct((3, 8, 128), jnp.float32)
    arguments = (
        positions.reshape(3, NT, 128),
        velocities.reshape(3, NT, 128),
        radius.reshape(NT, 128),
        group.reshape(NT, 128),
        broken.reshape(NT, 128),
        jnp.transpose(neighbours, (0, 1, 4, 2, 3)),
        counts.reshape(1, NT),
    )
    own, to_left, to_right, notes = pl.pallas_call(
        pack_kernel,
        out_shape=(tile, edge, edge, jax.ShapeDtypeStruct((8, 128), jnp.float32)),
        in_specs=[pl.BlockSpec(memory_space=pltpu.HBM)] * 7,
        out_specs=(VMEM,) * 4,
        scratch_shapes=[pltpu.VMEM(a.shape, a.dtype) for a in arguments] + [pltpu.SemaphoreType.DMA((7,))],
        name="pack",
    )(*arguments)
    from_left = shifted(to_right, "gx", 1, True)
    from_right = shifted(to_left, "gx", -1, True)
    line = jnp.concatenate([from_left, own, from_right], axis=0)
    width = NT + 6

    def extended(tiles):
        up = shifted(tiles, "gy", 1, False)
        down = shifted(tiles, "gy", -1, False)
        middle = jnp.concatenate([up, tiles, down], axis=0)
        low = shifted(middle, "gz", 1, True)
        high = shifted(middle, "gz", -1, True)
        return low, middle, high

    low, middle, high = extended(line)
    listed = [from_left[0, 0 : K + 1, NT - 1 : NT], notes[0 : K + 1, 0:NT], from_right[2, 0 : K + 1, 0:1]]
    listed = jnp.concatenate(listed, axis=1).astype(jnp.int32)
    spots = lax.broadcasted_iota(jnp.int32, (1, NT + 2), 1)
    shift = jnp.where(spots == 0, -1, jnp.where(spots == NT + 1, 1, 0))
    first_meta = list_entries(listed[0:K], listed[K:], spots + 2, shift, width, 3)
    spots = lax.broadcasted_iota(jnp.int32, (1, NT), 1)
    second_meta = list_entries(listed[0:K, 1 : NT + 1], listed[K:, 1 : NT + 1], spots + 1, 0, width - 4, 1)

    line = pl.pallas_call(
        first_kernel,
        out_shape=jax.ShapeDtypeStruct((width - 4, 8, 128), jnp.float32),
        in_specs=[SMEM] + [VMEM] * 3,
        out_specs=VMEM,
        scratch_shapes=[
            pltpu.VMEM((9 * width, 8, 128), jnp.float32),
            *work_space(),
        ],
        compiler_params=LARGE,
        name="first_step",
    )(first_meta, low, middle, high)
    low, middle, high = extended(line)
    width = width - 4
    peers = lax.axis_size("gx")
    block = jax.ShapeDtypeStruct((3, NT, 128), jnp.float32)
    places, speeds, grid, energy = pl.pallas_call(
        second_kernel,
        out_shape=(
            block,
            block,
            jax.ShapeDtypeStruct((64, 128), jnp.float32),
            jax.ShapeDtypeStruct((peers, 8, 128), jnp.float32),
        ),
        in_specs=[SMEM] + [VMEM] * 4,
        out_specs=(VMEM,) * 4,
        scratch_shapes=[
            pltpu.VMEM((9 * width, 8, 128), jnp.float32),
            pltpu.VMEM((64, NT * 128), jnp.bfloat16),
            pltpu.VMEM((256, NT * 128), jnp.bfloat16),
            pltpu.VMEM((8, 128), jnp.float32),
            *work_space(),
        ],
        compiler_params=LARGE,
        name="second_step",
    )(second_meta, cell.reshape(NT, 128), low, middle, high)
    energy = lax.all_to_all(energy, "gx", 0, 0, tiled=True)
    before = shifted(grid, "gx", 1, False)
    after = shifted(grid, "gx", -1, False)
    coords = jnp.stack([lax.axis_index(a) for a in ("gx", "gy", "gz")])
    rows = lax.axis_size("gy") * lax.axis_size("gz")
    parts = pl.pallas_call(
        plane_kernel,
        out_shape=jax.ShapeDtypeStruct((rows, 8, 128), jnp.float32),
        in_specs=[SMEM] + [VMEM] * 4,
        out_specs=VMEM,
        compiler_params=SMALL,
        name="planes",
    )(coords, grid, before, after, energy)
    parts = lax.all_to_all(parts, ("gy", "gz"), 0, 0, tiled=True)
    stress, motion, energies = pl.pallas_call(
        line_kernel,
        out_shape=(
            jax.ShapeDtypeStruct((6, 8, 64), jnp.float32),
            jax.ShapeDtypeStruct((4, 8, 64), jnp.float32),
            jax.ShapeDtypeStruct((3,), jnp.float32),
        ),
        in_specs=[VMEM],
        out_specs=(VMEM, VMEM, SMEM),
        compiler_params=SMALL,
        name="lines",
    )(parts)
    return (
        places.reshape(positions.shape),
        speeds.reshape(velocities.shape),
        stress.reshape(6, CX, 1, 64),
        motion.reshape(4, CX, 1, 64),
        energies,
    )


def solution(mesh):
    placed = (
        P(None, "gx", "gy", "gz", None),
        P(None, "gx", "gy", "gz", None),
        P("gx", "gy", "gz", None),
        P("gx", "gy", "gz", None),
        P("gx", "gy", "gz", None),
        P("gx", "gy", "gz", None),
        P("gx", "gy", "gz", None, None),
        P("gx", "gy", "gz", None),
    )
    return jax.shard_map(
        shards,
        mesh=mesh,
        in_specs=placed,
        out_specs=(
            P(None, "gx", "gy", "gz", None),
            P(None, "gx", "gy", "gz", None),
            P(None, "gx", ("gy", "gz"), None),
            P(None, "gx", ("gy", "gz"), None),
            P(),
        ),
        check_vma=False,
    )
```

```python
import math

import jax
import jax.numpy as jnp
from jax import lax
from jax.experimental import pallas as pl
from jax.experimental.pallas import tpu as pltpu
from jax.sharding import PartitionSpec as P

STEPS = 2
CX = 8
CY = 8
CZ = 8
SIGMA = 2
HW = 6
KN = 1.0
GAMMA = 1.0
KB = 2.0
REACH = 1.5
STEP_DT = 0.02
DENS = 4.0
SOFT = 0.0001

NT = 8
K = 6
FAR = -1.0e9
LIVE = 1024
INSIDE = 2048
ITSELF = 4096
COMPS = 10
VMEM = pl.BlockSpec(memory_space=pltpu.VMEM)
SMALL = pltpu.CompilerParams(vmem_limit_bytes=4 << 20)
LARGE = pltpu.CompilerParams(vmem_limit_bytes=10 << 20)
SMEM = pl.BlockSpec(memory_space=pltpu.SMEM)

RAW = [math.exp(-d * d / (2.0 * SIGMA * SIGMA)) for d in range(HW + 1)]
TOTAL = RAW[0] + 2.0 * sum(RAW[1:])
GAUSS = [w / TOTAL for w in RAW]


def twice(value):
    return jnp.concatenate([value, value], axis=0)


def own_columns(own, mine):
    for c in range(8):
        mine[c] = jnp.broadcast_to(own[c : c + 1, :], (128, 128)).T


def pair_sums(tiles, meta, t, own, second, rows, mine):
    lane = lax.broadcasted_iota(jnp.int32, (8, 128), 1).astype(jnp.float32)
    stride = meta.shape[0] // K
    for slot in range(K):
        entry = meta[slot * stride + t]
        index = lax.bitwise_and(entry, 1023)
        live = lax.bitwise_and(entry, LIVE) > 0
        for c in range(8 if slot < 3 else 7):
            value = jnp.broadcast_to(tiles[index, c : c + 1, :], (8, 128))
            if c == 6:
                value = jnp.where(jnp.logical_and(live, value > 0.0), value, FAR)
            if c == 7:
                value = jnp.where(lax.bitwise_and(entry, INSIDE) > 0, value, -7.0)
            rows[9 * slot + c] = value
        if second and slot < 3:
            rows[9 * slot + 8] = jnp.where(lax.bitwise_and(entry, ITSELF) > 0, lane, -1.0)
    own_columns(own, mine)
    number = lax.broadcasted_iota(jnp.int32, (16, 128), 0).astype(jnp.float32)
    count = 11 if second else 3
    stacks = []
    for block in range(8):
        xi, yi, zi, ui, vi, wi, ri, ci = [mine[c, 16 * block : 16 * block + 16, :] for c in range(8)]
        ci = jnp.where(ci < 0.0, -5.0, ci)
        here = number + float(16 * block)
        added = [jnp.zeros((16, 128), jnp.float32)] * count
        for slot in range(K):
            xj, yj, zj, uj, vj, wj, rj = [twice(rows[9 * slot + c]) for c in range(7)]
            dx, dy, dz = xj - xi, yj - yi, zj - zi
            square = dx * dx + dy * dy + (dz * dz + SOFT)
            inverse = lax.rsqrt(square)
            distance = square * inverse
            reach = rj + ri
            inter = jnp.maximum(reach - distance, 0.0)
            root = inter * lax.rsqrt(jnp.maximum(inter, 1e-30))
            closing = ((uj - ui) * dx + (vj - vi) * dy + (wj - wi) * dz) * inverse
            magnitude = root * (closing - inter)
            if slot < 3:
                ratio = lax.rsqrt(reach)
                window = jnp.maximum(1.0 - distance * ((1.0 / REACH) * ratio * ratio), 0.0)
                window = jnp.where(twice(rows[9 * slot + 7]) == ci, window * window, 0.0)
                stretch = distance - reach
                pull = stretch * window
                magnitude = magnitude + KB * pull
            scaled = magnitude * inverse
            fx, fy, fz = scaled * dx, scaled * dy, scaled * dz
            terms = [fx, fy, fz]
            if second:
                terms += [fx * dx, fy * dy, fz * dz, fx * dy, fx * dz, fy * dz]
                energy = inter * inter * root
                if slot < 3:
                    itself = twice(rows[9 * slot + 8]) == here
                    terms += [jnp.where(itself, 0.0, energy), jnp.where(itself, 0.0, pull * stretch)]
                else:
                    terms += [energy]
            added = [a + b for a, b in zip(added, terms)] + added[len(terms) :]
        stacks.append(added)
    totals = [jnp.concatenate([added[i] for added in stacks], axis=0).T for i in range(count)]
    return [jnp.sum(total, axis=0, keepdims=True) for total in totals]


def work_space():
    return (
        pltpu.VMEM((9 * K, 8, 128), jnp.float32),
        pltpu.VMEM((8, 128, 128), jnp.float32),
        pltpu.VMEM((9 * K, 8, 128), jnp.float32),
        pltpu.VMEM((8, 128, 128), jnp.float32),
    )


def fill(tiles, low, middle, high, size):
    for part, ref in enumerate((low, middle, high)):
        for i in range(size):
            tiles[part * size + i] = ref[i]


def first_kernel(meta, low, middle, high, out, tiles, *work):
    width = middle.shape[0] // 3
    fill(tiles, low, middle, high, 3 * width)
    sub = lax.broadcasted_iota(jnp.int32, (8, 128), 0)

    def one(t, *work):
        own = tiles[4 * width + t + 1]
        sums = pair_sums(tiles, meta, t, own, False, *work)
        radius = own[6:7, :]
        gain = STEP_DT / (DENS * radius * radius * radius)
        fresh = own
        for axis in range(3):
            speed = own[3 + axis : 4 + axis, :] + gain * sums[axis]
            place = own[axis : axis + 1, :] + STEP_DT * speed
            fresh = jnp.where(sub == axis, place, fresh)
            fresh = jnp.where(sub == 3 + axis, speed, fresh)
        out[t] = fresh

    @pl.loop(0, (width - 2) // 2)
    def _(t):
        one(2 * t, work[0], work[1])
        one(2 * t + 1, work[2], work[3])


def second_kernel(
    meta, low, middle, high, place_out, speed_out, values_out, energy_out, tiles, total, *work
):
    width = middle.shape[0] // 3
    fill(tiles, low, middle, high, 3 * width)
    sub = lax.broadcasted_iota(jnp.int32, (8, 128), 0)
    total[...] = jnp.zeros((8, 128), jnp.float32)

    def one(t, *work):
        own = tiles[4 * width + t + 1]
        sums = pair_sums(tiles, meta, t, own, True, *work)
        radius = own[6:7, :]
        mass = DENS * radius * radius * radius
        gain = STEP_DT / mass
        values = [-0.5 * sums[3 + i] for i in range(6)]
        squares = jnp.zeros((1, 128), jnp.float32)
        this = pl.ds(t, 1)
        for axis in range(3):
            speed = own[3 + axis : 4 + axis, :] + gain * sums[axis]
            speed_out[axis, this, :] = speed
            place_out[axis, this, :] = own[axis : axis + 1, :] + STEP_DT * speed
            squares = squares + speed * speed
            values.append(mass * speed)
        kinetic = 0.5 * mass * squares
        values.append(kinetic)
        contact = 0.4 * KN * sums[9]
        bond = 0.5 * KB * sums[10]
        added = jnp.where(sub == 0, kinetic, jnp.where(sub == 1, contact, jnp.where(sub == 2, bond, 0.0)))
        total[...] = total[...] + added
        for c in range(COMPS):
            values_out[t, c : c + 1, :] = values[c]

    @pl.loop(0, NT // 2)
    def _(t):
        one(2 * t, work[0], work[1])
        one(2 * t + 1, work[2], work[3])

    for i in range(energy_out.shape[0]):
        energy_out[i] = total[...]


def deposit_kernel(values, cell, grid, left, right):
    sub = lax.broadcasted_iota(jnp.int32, (8, 128), 0)
    line = lax.broadcasted_iota(jnp.int32, (64, 128), 0)
    right[...] = jnp.zeros(right.shape, jnp.bfloat16)
    for t in range(NT):
        where = cell[t : t + 1, :]
        span = slice(128 * t, 128 * t + 128)
        in_plane = sub == lax.shift_right_logical(where, 6)
        for c in range(0, COMPS, 2):
            pair = [jnp.where(in_plane, values[t, c + i : c + i + 1, :], 0.0) for i in range(2)]
            pair = jnp.concatenate(pair, axis=0)
            coarse = pair.astype(jnp.bfloat16)
            fine = (pair - coarse.astype(jnp.float32)).astype(jnp.bfloat16)
            right[8 * c : 8 * c + 16, span] = coarse
            right[128 + 8 * c : 128 + 8 * c + 16, span] = fine
        left[:, span] = jnp.where(line == lax.bitwise_and(where, 63), 1.0, 0.0).astype(jnp.bfloat16)
    both = lax.dot_general(
        left[...], right[...], (((1,), (1,)), ((), ())), preferred_element_type=jnp.float32
    )
    scale = float(CX * CY * CZ) / float(NT * 128)
    grid[...] = (both[:, 0:128] + both[:, 128:256]) * scale


def plane_kernel(coords, own, before, after, out):
    lane = lax.broadcasted_iota(jnp.int32, (8, 128), 1)
    inner = lax.bitwise_and(lane, 7)
    planes = []
    for y in range(CY):
        block = slice(8 * y, 8 * y + 8)
        here = own[block, :]
        low = pltpu.roll(before[block, :], 120, 1)
        high = pltpu.roll(after[block, :], 8, 1)
        smooth = GAUSS[0] * here
        for d in range(1, HW + 1):
            ahead = pltpu.roll(jnp.where(inner >= d, here, high), 128 - d, 1)
            behind = pltpu.roll(jnp.where(inner < 8 - d, here, low), d, 1)
            smooth = smooth + GAUSS[d] * (ahead + behind)
        planes.append(smooth)
    rows = out.shape[0]
    for j in range(rows):
        out[j] = jnp.zeros((8, 128), jnp.float32)
    start = coords[1] * CY
    for r in range(-HW, CY + HW):
        mixed = jnp.zeros((8, 128), jnp.float32)
        for y in range(CY):
            if abs(r - y) <= HW:
                mixed = mixed + GAUSS[abs(r - y)] * planes[y]

        @pl.when(jnp.logical_and(start + r >= 0, start + r < rows))
        def _():
            out[start + r] = mixed


def energy_kernel(parts, energy, out):
    lane = lax.broadcasted_iota(jnp.int32, (8, 128), 1)
    sums = energy[0]
    for i in range(1, energy.shape[0]):
        sums = sums + energy[i]
    sums = jnp.where(lane == 8 * COMPS, jnp.sum(sums, axis=1, keepdims=True), 0.0)
    for j in range(out.shape[0]):
        out[j] = parts[j] + sums


def line_kernel(parts, stress, motion, energies):
    count = parts.shape[0] // 8
    lane = lax.broadcasted_iota(jnp.int32, (8, 128), 1)
    sub = lax.broadcasted_iota(jnp.int32, (8, 128), 0)
    lines = []
    for block in range(8):
        line = parts[block]
        for other in range(1, count):
            line = line + parts[8 * other + block]
        lines.append(line)
    whole = lines[0]
    for line in lines[1:]:
        whole = whole + line
    for i in range(3):
        energies[i] = jnp.sum(jnp.where(jnp.logical_and(sub == i, lane == 8 * COMPS), whole, 0.0))
    empty = jnp.zeros((8, 128), jnp.float32)
    out = []
    for block in range(8):
        here = lines[block]
        low = lines[block - 1] if block > 0 else empty
        high = lines[block + 1] if block < 7 else empty
        smooth = GAUSS[0] * here
        for d in range(1, HW + 1):
            ahead = pltpu.roll(jnp.where(sub >= d, here, high), 8 - d, 0)
            behind = pltpu.roll(jnp.where(sub < 8 - d, here, low), d, 0)
            smooth = smooth + GAUSS[d] * (ahead + behind)
        out.append(smooth)
    turned = jnp.concatenate(out, axis=0).T
    for c in range(6):
        stress[c] = turned[8 * c : 8 * c + 8, :]
    for c in range(4):
        motion[c] = turned[48 + 8 * c : 56 + 8 * c, :]


def pack_kernel(*refs):
    sources, (out, to_left, to_right, notes), held, done = refs[0:7], refs[7:11], refs[11:18], refs[18]
    copies = [pltpu.make_async_copy(a, b, done.at[i]) for i, (a, b) in enumerate(zip(sources, held))]
    for copy in copies:
        copy.start()
    for copy in copies:
        copy.wait()
    place, speed, radius, group, broken, lists, counts = held
    code = jnp.where(broken[...] == 0, group[...].astype(jnp.float32), -1.0)
    for t in range(NT):
        for axis in range(3):
            out[t, axis : axis + 1, :] = place[axis, t : t + 1, :]
            out[t, 3 + axis : 4 + axis, :] = speed[axis, t : t + 1, :]
        out[t, 6:7, :] = radius[t : t + 1, :]
        out[t, 7:8, :] = code[t : t + 1, :]
    notes[...] = jnp.zeros((8, 128), jnp.float32)
    for slot in range(K):
        notes[slot : slot + 1, 1 : NT + 1] = lists[0, 0, slot].astype(jnp.float32)
    notes[K : K + 1, 1 : NT + 1] = counts[...].astype(jnp.float32)
    for ref, first in ((to_left, 0), (to_right, NT - 2)):
        ref[0] = out[first]
        ref[1] = out[first + 1]
        ref[2] = notes[...]


def join_kernel(left, own, right, mine, line, notes):
    for i in range(2):
        line[i] = left[i]
        line[NT + 2 + i] = right[i]
    for t in range(NT):
        line[2 + t] = own[t]
    lane = lax.broadcasted_iota(jnp.int32, (8, 128), 1)
    edges = jnp.where(lane == 0, pltpu.roll(left[2], 128 - NT, 1), pltpu.roll(right[2], NT, 1))
    notes[...] = jnp.where(jnp.logical_and(lane >= 1, lane <= NT), mine[...], edges)


def shifted(value, axis, step, wrap):
    count = lax.axis_size(axis)
    pairs = [(i, (i + step) % count) for i in range(count) if wrap or 0 <= i + step < count]
    return lax.ppermute(value, axis, pairs)


def list_entries(lists, counts, home, shift, width, margin):
    offset = lists // NT
    along = offset // 9 - 1
    across = offset // 3 % 3
    up = offset % 3
    spot = jnp.clip((along + shift) * NT + lists % NT + margin, 0, width - 1)

    def within(axis, step):
        moved = lax.axis_index(axis) + step
        return (moved >= 0) & (moved < lax.axis_size(axis))

    slot = lax.broadcasted_iota(jnp.int32, lists.shape, 0)
    live = (slot < counts) & within("gx", shift) & within("gx", shift + along)
    live = live & within("gy", across - 1) & within("gz", up - 1)
    inside = live & (offset == 13)
    itself = inside & (spot == home)
    entry = up * (3 * width) + across * width + spot
    entry = entry + LIVE * live.astype(jnp.int32) + INSIDE * inside.astype(jnp.int32)
    entry = entry + ITSELF * itself.astype(jnp.int32)
    own = inside.astype(jnp.int32)
    earlier = lax.broadcasted_iota(jnp.int32, (K, K, 1), 0) < lax.broadcasted_iota(jnp.int32, (K, K, 1), 1)
    before = jnp.sum(jnp.where(earlier, own[:, None, :], 0), axis=0)
    rank = jnp.where(inside, before, slot - before + jnp.sum(own, axis=0, keepdims=True))
    to = lax.broadcasted_iota(jnp.int32, (1, K, 1), 1)
    return jnp.sum(jnp.where(rank[:, None, :] == to, entry[:, None, :], 0), axis=0).reshape(-1)


def shards(positions, velocities, radius, group, broken, cell, neighbours, counts):
    tile = jax.ShapeDtypeStruct((NT, 8, 128), jnp.float32)
    edge = jax.ShapeDtypeStruct((3, 8, 128), jnp.float32)
    arguments = (
        positions.reshape(3, NT, 128),
        velocities.reshape(3, NT, 128),
        radius.reshape(NT, 128),
        group.reshape(NT, 128),
        broken.reshape(NT, 128),
        jnp.transpose(neighbours, (0, 1, 4, 2, 3)),
        counts.reshape(1, NT),
    )
    own, to_left, to_right, notes = pl.pallas_call(
        pack_kernel,
        out_shape=(tile, edge, edge, jax.ShapeDtypeStruct((8, 128), jnp.float32)),
        in_specs=[pl.BlockSpec(memory_space=pltpu.HBM)] * 7,
        out_specs=(VMEM,) * 4,
        scratch_shapes=[pltpu.VMEM(a.shape, a.dtype) for a in arguments] + [pltpu.SemaphoreType.DMA((7,))],
        name="pack",
    )(*arguments)
    from_left = shifted(to_right, "gx", 1, True)
    from_right = shifted(to_left, "gx", -1, True)
    width = NT + 4
    line, listed = pl.pallas_call(
        join_kernel,
        out_shape=(
            jax.ShapeDtypeStruct((width, 8, 128), jnp.float32),
            jax.ShapeDtypeStruct((8, 128), jnp.float32),
        ),
        in_specs=[VMEM] * 4,
        out_specs=(VMEM,) * 2,
        compiler_params=SMALL,
        name="join",
    )(from_left, own, from_right, notes)

    def extended(tiles):
        up = shifted(tiles, "gy", 1, False)
        down = shifted(tiles, "gy", -1, False)
        middle = jnp.concatenate([up, tiles, down], axis=0)
        low = shifted(middle, "gz", 1, True)
        high = shifted(middle, "gz", -1, True)
        return low, middle, high

    low, middle, high = extended(line)
    listed = listed[0 : K + 1, 0 : NT + 2].astype(jnp.int32)
    spots = lax.broadcasted_iota(jnp.int32, (1, NT + 2), 1)
    shift = jnp.where(spots == 0, -1, jnp.where(spots == NT + 1, 1, 0))
    first_meta = list_entries(listed[0:K], listed[K:], spots + 1, shift, width, 2)
    spots = lax.broadcasted_iota(jnp.int32, (1, NT), 1)
    second_meta = list_entries(listed[0:K, 1 : NT + 1], listed[K:, 1 : NT + 1], spots + 1, 0, width - 2, 1)

    line = pl.pallas_call(
        first_kernel,
        out_shape=jax.ShapeDtypeStruct((width - 2, 8, 128), jnp.float32),
        in_specs=[SMEM] + [VMEM] * 3,
        out_specs=VMEM,
        scratch_shapes=[
            pltpu.VMEM((9 * width, 8, 128), jnp.float32),
            *work_space(),
        ],
        compiler_params=LARGE,
        name="first_step",
    )(first_meta, low, middle, high)
    low, middle, high = extended(line)
    width = width - 2
    peers = lax.axis_size("gx")
    block = jax.ShapeDtypeStruct((3, NT, 128), jnp.float32)
    places, speeds, values, energy = pl.pallas_call(
        second_kernel,
        out_shape=(
            block,
            block,
            jax.ShapeDtypeStruct((NT, 16, 128), jnp.float32),
            jax.ShapeDtypeStruct((peers, 8, 128), jnp.float32),
        ),
        in_specs=[SMEM] + [VMEM] * 3,
        out_specs=(VMEM,) * 4,
        scratch_shapes=[
            pltpu.VMEM((9 * width, 8, 128), jnp.float32),
            pltpu.VMEM((8, 128), jnp.float32),
            *work_space(),
        ],
        compiler_params=LARGE,
        name="second_step",
    )(second_meta, low, middle, high)
    energy = lax.all_to_all(energy, "gx", 0, 0, tiled=True)
    grid = pl.pallas_call(
        deposit_kernel,
        out_shape=jax.ShapeDtypeStruct((64, 128), jnp.float32),
        in_specs=[VMEM] * 2,
        out_specs=VMEM,
        scratch_shapes=[
            pltpu.VMEM((64, NT * 128), jnp.bfloat16),
            pltpu.VMEM((256, NT * 128), jnp.bfloat16),
        ],
        compiler_params=SMALL,
        name="deposit",
    )(values, cell.reshape(NT, 128))
    before = shifted(grid, "gx", 1, False)
    after = shifted(grid, "gx", -1, False)
    coords = jnp.stack([lax.axis_index(a) for a in ("gx", "gy", "gz")])
    rows = lax.axis_size("gy") * lax.axis_size("gz")
    parts = pl.pallas_call(
        plane_kernel,
        out_shape=jax.ShapeDtypeStruct((rows, 8, 128), jnp.float32),
        in_specs=[SMEM] + [VMEM] * 3,
        out_specs=VMEM,
        compiler_params=SMALL,
        name="planes",
    )(coords, grid, before, after)
    parts = pl.pallas_call(
        energy_kernel,
        out_shape=jax.ShapeDtypeStruct((rows, 8, 128), jnp.float32),
        in_specs=[VMEM] * 2,
        out_specs=VMEM,
        compiler_params=SMALL,
        name="energies",
    )(parts, energy)
    parts = lax.all_to_all(parts, ("gy", "gz"), 0, 0, tiled=True)
    stress, motion, energies = pl.pallas_call(
        line_kernel,
        out_shape=(
            jax.ShapeDtypeStruct((6, 8, 64), jnp.float32),
            jax.ShapeDtypeStruct((4, 8, 64), jnp.float32),
            jax.ShapeDtypeStruct((3,), jnp.float32),
        ),
        in_specs=[VMEM],
        out_specs=(VMEM, VMEM, SMEM),
        compiler_params=SMALL,
        name="lines",
    )(parts)
    return (
        places.reshape(positions.shape),
        speeds.reshape(velocities.shape),
        stress.reshape(6, CX, 1, 64),
        motion.reshape(4, CX, 1, 64),
        energies,
    )


def solution(mesh):
    placed = (
        P(None, "gx", "gy", "gz", None),
        P(None, "gx", "gy", "gz", None),
        P("gx", "gy", "gz", None),
        P("gx", "gy", "gz", None),
        P("gx", "gy", "gz", None),
        P("gx", "gy", "gz", None),
        P("gx", "gy", "gz", None, None),
        P("gx", "gy", "gz", None),
    )
    return jax.shard_map(
        shards,
        mesh=mesh,
        in_specs=placed,
        out_specs=(
            P(None, "gx", "gy", "gz", None),
            P(None, "gx", "gy", "gz", None),
            P(None, "gx", ("gy", "gz"), None),
            P(None, "gx", ("gy", "gz"), None),
            P(),
        ),
        check_vma=False,
    )
```

```python
import math

import jax
import jax.numpy as jnp
from jax import lax
from jax.experimental import pallas as pl
from jax.experimental.pallas import tpu as pltpu
from jax.sharding import PartitionSpec as P

STEPS = 2
CX = 8
CY = 8
CZ = 8
SIGMA = 2
HW = 6
KN = 1.0
GAMMA = 1.0
KB = 2.0
REACH = 1.5
STEP_DT = 0.02
DENS = 4.0
SOFT = 0.0001

NT = 8
K = 6
FAR = -1.0e9
LIVE = 1024
INSIDE = 2048
ITSELF = 4096
COMPS = 10
VMEM = pl.BlockSpec(memory_space=pltpu.VMEM)
SMALL = pltpu.CompilerParams(vmem_limit_bytes=4 << 20)
LARGE = pltpu.CompilerParams(vmem_limit_bytes=10 << 20)
SMEM = pl.BlockSpec(memory_space=pltpu.SMEM)

RAW = [math.exp(-d * d / (2.0 * SIGMA * SIGMA)) for d in range(HW + 1)]
TOTAL = RAW[0] + 2.0 * sum(RAW[1:])
GAUSS = [w / TOTAL for w in RAW]


def twice(value):
    return jnp.concatenate([value, value], axis=0)


def turn_kernel(middle, out):
    width = middle.shape[0] // 3

    @pl.loop(0, out.shape[0])
    def _(t):
        own = middle[width + 1 + t]
        for c in range(8):
            out[t, c] = jnp.broadcast_to(own[c : c + 1, :], (128, 128)).T


def turned(middle, count):
    return pl.pallas_call(
        turn_kernel,
        out_shape=jax.ShapeDtypeStruct((count, 8, 128, 128), jnp.float32),
        in_specs=[VMEM],
        out_specs=VMEM,
        compiler_params=SMALL,
        cost_estimate=pl.CostEstimate(flops=0, bytes_accessed=count * (8 << 16), transcendentals=0),
        name="turn",
    )(middle)


def pair_sums(tiles, meta, t, second, rows, mine):
    lane = lax.broadcasted_iota(jnp.int32, (8, 128), 1).astype(jnp.float32)
    stride = meta.shape[0] // K
    for slot in range(K):
        entry = meta[slot * stride + t]
        index = lax.bitwise_and(entry, 1023)
        live = lax.bitwise_and(entry, LIVE) > 0
        for c in range(8 if slot < 3 else 7):
            value = jnp.broadcast_to(tiles[index, c : c + 1, :], (8, 128))
            if c == 6:
                value = jnp.where(jnp.logical_and(live, value > 0.0), value, FAR)
            if c == 7:
                value = jnp.where(lax.bitwise_and(entry, INSIDE) > 0, value, -7.0)
            rows[9 * slot + c] = value
        if second and slot < 3:
            rows[9 * slot + 8] = jnp.where(lax.bitwise_and(entry, ITSELF) > 0, lane, -1.0)
    number = lax.broadcasted_iota(jnp.int32, (16, 128), 0).astype(jnp.float32)
    count = 11 if second else 3
    stacks = []
    for block in range(8):
        xi, yi, zi, ui, vi, wi, ri, ci = [mine[t, c, 16 * block : 16 * block + 16, :] for c in range(8)]
        ci = jnp.where(ci < 0.0, -5.0, ci)
        here = number + float(16 * block)
        added = [jnp.zeros((16, 128), jnp.float32)] * count
        for slot in range(K):
            xj, yj, zj, uj, vj, wj, rj = [twice(rows[9 * slot + c]) for c in range(7)]
            dx, dy, dz = xj - xi, yj - yi, zj - zi
            square = dx * dx + dy * dy + (dz * dz + SOFT)
            inverse = lax.rsqrt(square)
            distance = square * inverse
            reach = rj + ri
            inter = jnp.maximum(reach - distance, 0.0)
            root = inter * lax.rsqrt(jnp.maximum(inter, 1e-30))
            closing = ((uj - ui) * dx + (vj - vi) * dy + (wj - wi) * dz) * inverse
            magnitude = root * (closing - inter)
            if slot < 3:
                ratio = lax.rsqrt(reach)
                window = jnp.maximum(1.0 - distance * ((1.0 / REACH) * ratio * ratio), 0.0)
                window = jnp.where(twice(rows[9 * slot + 7]) == ci, window * window, 0.0)
                stretch = distance - reach
                pull = stretch * window
                magnitude = magnitude + KB * pull
            scaled = magnitude * inverse
            fx, fy, fz = scaled * dx, scaled * dy, scaled * dz
            terms = [fx, fy, fz]
            if second:
                terms += [fx * dx, fy * dy, fz * dz, fx * dy, fx * dz, fy * dz]
                energy = inter * inter * root
                if slot < 3:
                    itself = twice(rows[9 * slot + 8]) == here
                    terms += [jnp.where(itself, 0.0, energy), jnp.where(itself, 0.0, pull * stretch)]
                else:
                    terms += [energy]
            added = [a + b for a, b in zip(added, terms)] + added[len(terms) :]
        stacks.append(added)
    totals = [jnp.concatenate([added[i] for added in stacks], axis=0).T for i in range(count)]
    return [jnp.sum(total, axis=0, keepdims=True) for total in totals]


def work_space():
    return (pltpu.VMEM((9 * K, 8, 128), jnp.float32), pltpu.VMEM((9 * K, 8, 128), jnp.float32))


def fill(tiles, low, middle, high, size):
    for part, ref in enumerate((low, middle, high)):
        for i in range(size):
            tiles[part * size + i] = ref[i]


def first_kernel(meta, low, middle, high, mine, out, tiles, *work):
    width = middle.shape[0] // 3
    fill(tiles, low, middle, high, 3 * width)
    sub = lax.broadcasted_iota(jnp.int32, (8, 128), 0)

    def one(t, rows):
        own = tiles[4 * width + t + 1]
        sums = pair_sums(tiles, meta, t, False, rows, mine)
        radius = own[6:7, :]
        gain = STEP_DT / (DENS * radius * radius * radius)
        fresh = own
        for axis in range(3):
            speed = own[3 + axis : 4 + axis, :] + gain * sums[axis]
            place = own[axis : axis + 1, :] + STEP_DT * speed
            fresh = jnp.where(sub == axis, place, fresh)
            fresh = jnp.where(sub == 3 + axis, speed, fresh)
        out[t] = fresh

    @pl.loop(0, (width - 2) // 2)
    def _(t):
        one(2 * t, work[0])
        one(2 * t + 1, work[1])


def second_kernel(
    meta, low, middle, high, mine, place_out, speed_out, values_out, energy_out, tiles, total, *work
):
    width = middle.shape[0] // 3
    fill(tiles, low, middle, high, 3 * width)
    sub = lax.broadcasted_iota(jnp.int32, (8, 128), 0)
    total[...] = jnp.zeros((8, 128), jnp.float32)

    def one(t, rows):
        own = tiles[4 * width + t + 1]
        sums = pair_sums(tiles, meta, t, True, rows, mine)
        radius = own[6:7, :]
        mass = DENS * radius * radius * radius
        gain = STEP_DT / mass
        values = [-0.5 * sums[3 + i] for i in range(6)]
        squares = jnp.zeros((1, 128), jnp.float32)
        this = pl.ds(t, 1)
        for axis in range(3):
            speed = own[3 + axis : 4 + axis, :] + gain * sums[axis]
            speed_out[axis, this, :] = speed
            place_out[axis, this, :] = own[axis : axis + 1, :] + STEP_DT * speed
            squares = squares + speed * speed
            values.append(mass * speed)
        kinetic = 0.5 * mass * squares
        values.append(kinetic)
        contact = 0.4 * KN * sums[9]
        bond = 0.5 * KB * sums[10]
        added = jnp.where(sub == 0, kinetic, jnp.where(sub == 1, contact, jnp.where(sub == 2, bond, 0.0)))
        total[...] = total[...] + added
        for c in range(COMPS):
            values_out[t, c : c + 1, :] = values[c]

    @pl.loop(0, NT // 2)
    def _(t):
        one(2 * t, work[0])
        one(2 * t + 1, work[1])

    for i in range(energy_out.shape[0]):
        energy_out[i] = total[...]


def deposit_kernel(values, cell, grid, left, right):
    sub = lax.broadcasted_iota(jnp.int32, (8, 128), 0)
    line = lax.broadcasted_iota(jnp.int32, (64, 128), 0)
    right[...] = jnp.zeros(right.shape, jnp.bfloat16)
    for t in range(NT):
        where = cell[t : t + 1, :]
        span = slice(128 * t, 128 * t + 128)
        in_plane = sub == lax.shift_right_logical(where, 6)
        for c in range(0, COMPS, 2):
            pair = [jnp.where(in_plane, values[t, c + i : c + i + 1, :], 0.0) for i in range(2)]
            pair = jnp.concatenate(pair, axis=0)
            coarse = pair.astype(jnp.bfloat16)
            fine = (pair - coarse.astype(jnp.float32)).astype(jnp.bfloat16)
            right[8 * c : 8 * c + 16, span] = coarse
            right[128 + 8 * c : 128 + 8 * c + 16, span] = fine
        left[:, span] = jnp.where(line == lax.bitwise_and(where, 63), 1.0, 0.0).astype(jnp.bfloat16)
    both = lax.dot_general(
        left[...], right[...], (((1,), (1,)), ((), ())), preferred_element_type=jnp.float32
    )
    scale = float(CX * CY * CZ) / float(NT * 128)
    grid[...] = (both[:, 0:128] + both[:, 128:256]) * scale


def plane_kernel(coords, own, before, after, out):
    lane = lax.broadcasted_iota(jnp.int32, (8, 128), 1)
    inner = lax.bitwise_and(lane, 7)
    planes = []
    for y in range(CY):
        block = slice(8 * y, 8 * y + 8)
        here = own[block, :]
        low = pltpu.roll(before[block, :], 120, 1)
        high = pltpu.roll(after[block, :], 8, 1)
        smooth = GAUSS[0] * here
        for d in range(1, HW + 1):
            ahead = pltpu.roll(jnp.where(inner >= d, here, high), 128 - d, 1)
            behind = pltpu.roll(jnp.where(inner < 8 - d, here, low), d, 1)
            smooth = smooth + GAUSS[d] * (ahead + behind)
        planes.append(smooth)
    rows = out.shape[0]
    for j in range(rows):
        out[j] = jnp.zeros((8, 128), jnp.float32)
    start = coords[1] * CY
    for r in range(-HW, CY + HW):
        mixed = jnp.zeros((8, 128), jnp.float32)
        for y in range(CY):
            if abs(r - y) <= HW:
                mixed = mixed + GAUSS[abs(r - y)] * planes[y]

        @pl.when(jnp.logical_and(start + r >= 0, start + r < rows))
        def _():
            out[start + r] = mixed


def energy_kernel(parts, energy, out):
    lane = lax.broadcasted_iota(jnp.int32, (8, 128), 1)
    sums = energy[0]
    for i in range(1, energy.shape[0]):
        sums = sums + energy[i]
    sums = jnp.where(lane == 8 * COMPS, jnp.sum(sums, axis=1, keepdims=True), 0.0)
    for j in range(out.shape[0]):
        out[j] = parts[j] + sums


def line_kernel(parts, stress, motion, energies):
    count = parts.shape[0] // 8
    lane = lax.broadcasted_iota(jnp.int32, (8, 128), 1)
    sub = lax.broadcasted_iota(jnp.int32, (8, 128), 0)
    lines = []
    for block in range(8):
        line = parts[block]
        for other in range(1, count):
            line = line + parts[8 * other + block]
        lines.append(line)
    whole = lines[0]
    for line in lines[1:]:
        whole = whole + line
    for i in range(3):
        energies[i] = jnp.sum(jnp.where(jnp.logical_and(sub == i, lane == 8 * COMPS), whole, 0.0))
    empty = jnp.zeros((8, 128), jnp.float32)
    out = []
    for block in range(8):
        here = lines[block]
        low = lines[block - 1] if block > 0 else empty
        high = lines[block + 1] if block < 7 else empty
        smooth = GAUSS[0] * here
        for d in range(1, HW + 1):
            ahead = pltpu.roll(jnp.where(sub >= d, here, high), 8 - d, 0)
            behind = pltpu.roll(jnp.where(sub < 8 - d, here, low), d, 0)
            smooth = smooth + GAUSS[d] * (ahead + behind)
        out.append(smooth)
    turned = jnp.concatenate(out, axis=0).T
    for c in range(6):
        stress[c] = turned[8 * c : 8 * c + 8, :]
    for c in range(4):
        motion[c] = turned[48 + 8 * c : 56 + 8 * c, :]


def pack_kernel(*refs):
    sources, (out, to_left, to_right, notes), held, done = refs[0:7], refs[7:11], refs[11:18], refs[18]
    copies = [pltpu.make_async_copy(a, b, done.at[i]) for i, (a, b) in enumerate(zip(sources, held))]
    for copy in copies:
        copy.start()
    for copy in copies:
        copy.wait()
    place, speed, radius, group, broken, lists, counts = held
    code = jnp.where(broken[...] == 0, group[...].astype(jnp.float32), -1.0)
    for t in range(NT):
        for axis in range(3):
            out[t, axis : axis + 1, :] = place[axis, t : t + 1, :]
            out[t, 3 + axis : 4 + axis, :] = speed[axis, t : t + 1, :]
        out[t, 6:7, :] = radius[t : t + 1, :]
        out[t, 7:8, :] = code[t : t + 1, :]
    notes[...] = jnp.zeros((8, 128), jnp.float32)
    for slot in range(K):
        notes[slot : slot + 1, 1 : NT + 1] = lists[0, 0, slot].astype(jnp.float32)
    notes[K : K + 1, 1 : NT + 1] = counts[...].astype(jnp.float32)
    for ref, first in ((to_left, 0), (to_right, NT - 2)):
        ref[0] = out[first]
        ref[1] = out[first + 1]
        ref[2] = notes[...]


def keep_kernel(own, notes, own_out, notes_out):
    own_out[...] = own[...]
    notes_out[...] = notes[...]


def join_kernel(left, own, right, mine, line, notes):
    for i in range(2):
        line[i] = left[i]
        line[NT + 2 + i] = right[i]
    for t in range(NT):
        line[2 + t] = own[t]
    lane = lax.broadcasted_iota(jnp.int32, (8, 128), 1)
    edges = jnp.where(lane == 0, pltpu.roll(left[2], 128 - NT, 1), pltpu.roll(right[2], NT, 1))
    notes[...] = jnp.where(jnp.logical_and(lane >= 1, lane <= NT), mine[...], edges)


def shifted(value, axis, step, wrap):
    count = lax.axis_size(axis)
    pairs = [(i, (i + step) % count) for i in range(count) if wrap or 0 <= i + step < count]
    return lax.ppermute(value, axis, pairs)


def list_entries(lists, counts, home, shift, width, margin):
    offset = lists // NT
    along = offset // 9 - 1
    across = offset // 3 % 3
    up = offset % 3
    spot = jnp.clip((along + shift) * NT + lists % NT + margin, 0, width - 1)

    def within(axis, step):
        moved = lax.axis_index(axis) + step
        return (moved >= 0) & (moved < lax.axis_size(axis))

    slot = lax.broadcasted_iota(jnp.int32, lists.shape, 0)
    live = (slot < counts) & within("gx", shift) & within("gx", shift + along)
    live = live & within("gy", across - 1) & within("gz", up - 1)
    inside = live & (offset == 13)
    itself = inside & (spot == home)
    entry = up * (3 * width) + across * width + spot
    entry = entry + LIVE * live.astype(jnp.int32) + INSIDE * inside.astype(jnp.int32)
    entry = entry + ITSELF * itself.astype(jnp.int32)
    own = inside.astype(jnp.int32)
    earlier = lax.broadcasted_iota(jnp.int32, (K, K, 1), 0) < lax.broadcasted_iota(jnp.int32, (K, K, 1), 1)
    before = jnp.sum(jnp.where(earlier, own[:, None, :], 0), axis=0)
    rank = jnp.where(inside, before, slot - before + jnp.sum(own, axis=0, keepdims=True))
    to = lax.broadcasted_iota(jnp.int32, (1, K, 1), 1)
    return jnp.sum(jnp.where(rank[:, None, :] == to, entry[:, None, :], 0), axis=0).reshape(-1)


def shards(positions, velocities, radius, group, broken, cell, neighbours, counts):
    tile = jax.ShapeDtypeStruct((NT, 8, 128), jnp.float32)
    edge = jax.ShapeDtypeStruct((3, 8, 128), jnp.float32)
    arguments = (
        positions.reshape(3, NT, 128),
        velocities.reshape(3, NT, 128),
        radius.reshape(NT, 128),
        group.reshape(NT, 128),
        broken.reshape(NT, 128),
        jnp.transpose(neighbours, (0, 1, 4, 2, 3)),
        counts.reshape(1, NT),
    )
    own, to_left, to_right, notes = pl.pallas_call(
        pack_kernel,
        out_shape=(tile, edge, edge, jax.ShapeDtypeStruct((8, 128), jnp.float32)),
        in_specs=[pl.BlockSpec(memory_space=pltpu.HBM)] * 7,
        out_specs=(VMEM,) * 4,
        scratch_shapes=[pltpu.VMEM(a.shape, a.dtype) for a in arguments] + [pltpu.SemaphoreType.DMA((7,))],
        name="pack",
    )(*arguments)
    own, notes = pl.pallas_call(
        keep_kernel,
        out_shape=(tile, jax.ShapeDtypeStruct((8, 128), jnp.float32)),
        in_specs=[VMEM] * 2,
        out_specs=(VMEM,) * 2,
        compiler_params=SMALL,
        cost_estimate=pl.CostEstimate(flops=0, bytes_accessed=2 << 20, transcendentals=0),
        name="keep",
    )(own, notes)
    from_left = shifted(to_right, "gx", 1, True)
    from_right = shifted(to_left, "gx", -1, True)
    width = NT + 4
    line, listed = pl.pallas_call(
        join_kernel,
        out_shape=(
            jax.ShapeDtypeStruct((width, 8, 128), jnp.float32),
            jax.ShapeDtypeStruct((8, 128), jnp.float32),
        ),
        in_specs=[VMEM] * 4,
        out_specs=(VMEM,) * 2,
        compiler_params=SMALL,
        name="join",
    )(from_left, own, from_right, notes)

    def extended(tiles):
        up = shifted(tiles, "gy", 1, False)
        down = shifted(tiles, "gy", -1, False)
        middle = jnp.concatenate([up, tiles, down], axis=0)
        low = shifted(middle, "gz", 1, True)
        high = shifted(middle, "gz", -1, True)
        return low, middle, high

    low, middle, high = extended(line)
    mine = turned(middle, width - 2)
    listed = listed[0 : K + 1, 0 : NT + 2].astype(jnp.int32)
    spots = lax.broadcasted_iota(jnp.int32, (1, NT + 2), 1)
    shift = jnp.where(spots == 0, -1, jnp.where(spots == NT + 1, 1, 0))
    first_meta = list_entries(listed[0:K], listed[K:], spots + 1, shift, width, 2)
    spots = lax.broadcasted_iota(jnp.int32, (1, NT), 1)
    second_meta = list_entries(listed[0:K, 1 : NT + 1], listed[K:, 1 : NT + 1], spots + 1, 0, width - 2, 1)

    line = pl.pallas_call(
        first_kernel,
        out_shape=jax.ShapeDtypeStruct((width - 2, 8, 128), jnp.float32),
        in_specs=[SMEM] + [VMEM] * 4,
        out_specs=VMEM,
        scratch_shapes=[
            pltpu.VMEM((9 * width, 8, 128), jnp.float32),
            *work_space(),
        ],
        compiler_params=LARGE,
        name="first_step",
    )(first_meta, low, middle, high, mine)
    low, middle, high = extended(line)
    mine = turned(middle, NT)
    width = width - 2
    peers = lax.axis_size("gx")
    block = jax.ShapeDtypeStruct((3, NT, 128), jnp.float32)
    places, speeds, values, energy = pl.pallas_call(
        second_kernel,
        out_shape=(
            block,
            block,
            jax.ShapeDtypeStruct((NT, 16, 128), jnp.float32),
            jax.ShapeDtypeStruct((peers, 8, 128), jnp.float32),
        ),
        in_specs=[SMEM] + [VMEM] * 4,
        out_specs=(VMEM,) * 4,
        scratch_shapes=[
            pltpu.VMEM((9 * width, 8, 128), jnp.float32),
            pltpu.VMEM((8, 128), jnp.float32),
            *work_space(),
        ],
        compiler_params=LARGE,
        name="second_step",
    )(second_meta, low, middle, high, mine)
    energy = lax.all_to_all(energy, "gx", 0, 0, tiled=True)
    grid = pl.pallas_call(
        deposit_kernel,
        out_shape=jax.ShapeDtypeStruct((64, 128), jnp.float32),
        in_specs=[VMEM] * 2,
        out_specs=VMEM,
        scratch_shapes=[
            pltpu.VMEM((64, NT * 128), jnp.bfloat16),
            pltpu.VMEM((256, NT * 128), jnp.bfloat16),
        ],
        compiler_params=SMALL,
        name="deposit",
    )(values, cell.reshape(NT, 128))
    before = shifted(grid, "gx", 1, False)
    after = shifted(grid, "gx", -1, False)
    coords = jnp.stack([lax.axis_index(a) for a in ("gx", "gy", "gz")])
    rows = lax.axis_size("gy") * lax.axis_size("gz")
    parts = pl.pallas_call(
        plane_kernel,
        out_shape=jax.ShapeDtypeStruct((rows, 8, 128), jnp.float32),
        in_specs=[SMEM] + [VMEM] * 3,
        out_specs=VMEM,
        compiler_params=SMALL,
        name="planes",
    )(coords, grid, before, after)
    parts = pl.pallas_call(
        energy_kernel,
        out_shape=jax.ShapeDtypeStruct((rows, 8, 128), jnp.float32),
        in_specs=[VMEM] * 2,
        out_specs=VMEM,
        compiler_params=SMALL,
        name="energies",
    )(parts, energy)
    parts = lax.all_to_all(parts, ("gy", "gz"), 0, 0, tiled=True)
    stress, motion, energies = pl.pallas_call(
        line_kernel,
        out_shape=(
            jax.ShapeDtypeStruct((6, 8, 64), jnp.float32),
            jax.ShapeDtypeStruct((4, 8, 64), jnp.float32),
            jax.ShapeDtypeStruct((3,), jnp.float32),
        ),
        in_specs=[VMEM],
        out_specs=(VMEM, VMEM, SMEM),
        compiler_params=SMALL,
        name="lines",
    )(parts)
    return (
        places.reshape(positions.shape),
        speeds.reshape(velocities.shape),
        stress.reshape(6, CX, 1, 64),
        motion.reshape(4, CX, 1, 64),
        energies,
    )


def solution(mesh):
    placed = (
        P(None, "gx", "gy", "gz", None),
        P(None, "gx", "gy", "gz", None),
        P("gx", "gy", "gz", None),
        P("gx", "gy", "gz", None),
        P("gx", "gy", "gz", None),
        P("gx", "gy", "gz", None),
        P("gx", "gy", "gz", None, None),
        P("gx", "gy", "gz", None),
    )
    return jax.shard_map(
        shards,
        mesh=mesh,
        in_specs=placed,
        out_specs=(
            P(None, "gx", "gy", "gz", None),
            P(None, "gx", "gy", "gz", None),
            P(None, "gx", ("gy", "gz"), None),
            P(None, "gx", ("gy", "gz"), None),
            P(),
        ),
        check_vma=False,
    )
```

```python
import math

import jax
import jax.numpy as jnp
from jax import lax
from jax.experimental import pallas as pl
from jax.experimental.pallas import tpu as pltpu
from jax.sharding import PartitionSpec as P

STEPS = 2
CX = 8
CY = 8
CZ = 8
SIGMA = 2
HW = 6
KN = 1.0
GAMMA = 1.0
KB = 2.0
REACH = 1.5
STEP_DT = 0.02
DENS = 4.0
SOFT = 0.0001

NT = 8
K = 6
FAR = -1.0e9
LIVE = 1024
INSIDE = 2048
ITSELF = 4096
COMPS = 10
GROUP = 5
VMEM = pl.BlockSpec(memory_space=pltpu.VMEM)
SMALL = pltpu.CompilerParams(vmem_limit_bytes=4 << 20)
LARGE = pltpu.CompilerParams(vmem_limit_bytes=10 << 20)
SMEM = pl.BlockSpec(memory_space=pltpu.SMEM)

RAW = [math.exp(-d * d / (2.0 * SIGMA * SIGMA)) for d in range(HW + 1)]
TOTAL = RAW[0] + 2.0 * sum(RAW[1:])
GAUSS = [w / TOTAL for w in RAW]


def twice(value):
    return jnp.concatenate([value, value], axis=0)


def turn_kernel(middle, out):
    width = middle.shape[0] // 3

    @pl.loop(0, out.shape[0])
    def _(t):
        own = middle[width + 1 + t]
        for c in range(8):
            out[t, c] = jnp.broadcast_to(own[c : c + 1, :], (128, 128)).T


def turned(middle, count):
    return pl.pallas_call(
        turn_kernel,
        out_shape=jax.ShapeDtypeStruct((count, 8, 128, 128), jnp.float32),
        in_specs=[VMEM],
        out_specs=VMEM,
        compiler_params=SMALL,
        cost_estimate=pl.CostEstimate(flops=0, bytes_accessed=count * (8 << 16), transcendentals=0),
        name="turn",
    )(middle)


def pair_sums(tiles, meta, t, second, rows, mine):
    lane = lax.broadcasted_iota(jnp.int32, (8, 128), 1).astype(jnp.float32)
    stride = meta.shape[0] // K
    for slot in range(K):
        entry = meta[slot * stride + t]
        index = lax.bitwise_and(entry, 1023)
        live = lax.bitwise_and(entry, LIVE) > 0
        for c in range(8 if slot < 3 else 7):
            value = jnp.broadcast_to(tiles[index, c : c + 1, :], (8, 128))
            if c == 6:
                value = jnp.where(jnp.logical_and(live, value > 0.0), value, FAR)
            if c == 7:
                value = jnp.where(lax.bitwise_and(entry, INSIDE) > 0, value, -7.0)
            rows[9 * slot + c] = value
        if second and slot < 3:
            rows[9 * slot + 8] = jnp.where(lax.bitwise_and(entry, ITSELF) > 0, lane, -1.0)
    number = lax.broadcasted_iota(jnp.int32, (16, 128), 0).astype(jnp.float32)
    count = 11 if second else 3
    stacks = []
    for block in range(8):
        xi, yi, zi, ui, vi, wi, ri, ci = [mine[t, c, 16 * block : 16 * block + 16, :] for c in range(8)]
        ci = jnp.where(ci < 0.0, -5.0, ci)
        here = number + float(16 * block)
        added = [jnp.zeros((16, 128), jnp.float32)] * count
        for slot in range(K):
            xj, yj, zj, uj, vj, wj, rj = [twice(rows[9 * slot + c]) for c in range(7)]
            dx, dy, dz = xj - xi, yj - yi, zj - zi
            square = dx * dx + dy * dy + (dz * dz + SOFT)
            inverse = lax.rsqrt(square)
            distance = square * inverse
            reach = rj + ri
            inter = jnp.maximum(reach - distance, 0.0)
            root = inter * lax.rsqrt(jnp.maximum(inter, 1e-30))
            closing = ((uj - ui) * dx + (vj - vi) * dy + (wj - wi) * dz) * inverse
            magnitude = root * (closing - inter)
            if slot < 3:
                ratio = lax.rsqrt(reach)
                window = jnp.maximum(1.0 - distance * ((1.0 / REACH) * ratio * ratio), 0.0)
                window = jnp.where(twice(rows[9 * slot + 7]) == ci, window * window, 0.0)
                stretch = distance - reach
                pull = stretch * window
                magnitude = magnitude + KB * pull
            scaled = magnitude * inverse
            fx, fy, fz = scaled * dx, scaled * dy, scaled * dz
            terms = [fx, fy, fz]
            if second:
                terms += [fx * dx, fy * dy, fz * dz, fx * dy, fx * dz, fy * dz]
                energy = inter * inter * root
                if slot < 3:
                    itself = twice(rows[9 * slot + 8]) == here
                    terms += [jnp.where(itself, 0.0, energy), jnp.where(itself, 0.0, pull * stretch)]
                else:
                    terms += [energy]
            added = [a + b for a, b in zip(added, terms)] + added[len(terms) :]
        stacks.append(added)
    totals = [jnp.concatenate([added[i] for added in stacks], axis=0).T for i in range(count)]
    return [jnp.sum(total, axis=0, keepdims=True) for total in totals]


def work_space():
    return (pltpu.VMEM((9 * K, 8, 128), jnp.float32),) * GROUP


def fill(tiles, low, middle, high, size):
    for part, ref in enumerate((low, middle, high)):
        for i in range(size):
            tiles[part * size + i] = ref[i]


def first_kernel(meta, low, middle, high, mine, out, tiles, *work):
    width = middle.shape[0] // 3
    fill(tiles, low, middle, high, 3 * width)
    sub = lax.broadcasted_iota(jnp.int32, (8, 128), 0)

    def one(t, rows):
        own = tiles[4 * width + t + 1]
        sums = pair_sums(tiles, meta, t, False, rows, mine)
        radius = own[6:7, :]
        gain = STEP_DT / (DENS * radius * radius * radius)
        fresh = own
        for axis in range(3):
            speed = own[3 + axis : 4 + axis, :] + gain * sums[axis]
            place = own[axis : axis + 1, :] + STEP_DT * speed
            fresh = jnp.where(sub == axis, place, fresh)
            fresh = jnp.where(sub == 3 + axis, speed, fresh)
        out[t] = fresh

    @pl.loop(0, (width - 2) // GROUP)
    def _(t):
        for i in range(GROUP):
            one(GROUP * t + i, work[i])


def second_kernel(
    meta, low, middle, high, mine, place_out, speed_out, values_out, energy_out, tiles, total, *work
):
    width = middle.shape[0] // 3
    fill(tiles, low, middle, high, 3 * width)
    sub = lax.broadcasted_iota(jnp.int32, (8, 128), 0)
    total[...] = jnp.zeros((8, 128), jnp.float32)

    def one(t, rows):
        own = tiles[4 * width + t + 1]
        sums = pair_sums(tiles, meta, t, True, rows, mine)
        radius = own[6:7, :]
        mass = DENS * radius * radius * radius
        gain = STEP_DT / mass
        values = [-0.5 * sums[3 + i] for i in range(6)]
        squares = jnp.zeros((1, 128), jnp.float32)
        this = pl.ds(t, 1)
        for axis in range(3):
            speed = own[3 + axis : 4 + axis, :] + gain * sums[axis]
            speed_out[axis, this, :] = speed
            place_out[axis, this, :] = own[axis : axis + 1, :] + STEP_DT * speed
            squares = squares + speed * speed
            values.append(mass * speed)
        kinetic = 0.5 * mass * squares
        values.append(kinetic)
        contact = 0.4 * KN * sums[9]
        bond = 0.5 * KB * sums[10]
        added = jnp.where(sub == 0, kinetic, jnp.where(sub == 1, contact, jnp.where(sub == 2, bond, 0.0)))
        total[...] = total[...] + added
        for c in range(COMPS):
            values_out[t, c : c + 1, :] = values[c]

    @pl.loop(0, NT // 4)
    def _(t):
        for i in range(4):
            one(4 * t + i, work[i])

    for i in range(energy_out.shape[0]):
        energy_out[i] = total[...]


def deposit_kernel(values, cell, grid, left, right):
    sub = lax.broadcasted_iota(jnp.int32, (8, 128), 0)
    line = lax.broadcasted_iota(jnp.int32, (64, 128), 0)
    right[...] = jnp.zeros(right.shape, jnp.bfloat16)
    for t in range(NT):
        where = cell[t : t + 1, :]
        span = slice(128 * t, 128 * t + 128)
        in_plane = sub == lax.shift_right_logical(where, 6)
        for c in range(0, COMPS, 2):
            pair = [jnp.where(in_plane, values[t, c + i : c + i + 1, :], 0.0) for i in range(2)]
            pair = jnp.concatenate(pair, axis=0)
            coarse = pair.astype(jnp.bfloat16)
            fine = (pair - coarse.astype(jnp.float32)).astype(jnp.bfloat16)
            right[8 * c : 8 * c + 16, span] = coarse
            right[128 + 8 * c : 128 + 8 * c + 16, span] = fine
        left[:, span] = jnp.where(line == lax.bitwise_and(where, 63), 1.0, 0.0).astype(jnp.bfloat16)
    both = lax.dot_general(
        left[...], right[...], (((1,), (1,)), ((), ())), preferred_element_type=jnp.float32
    )
    scale = float(CX * CY * CZ) / float(NT * 128)
    grid[...] = (both[:, 0:128] + both[:, 128:256]) * scale


def plane_kernel(coords, own, before, after, out):
    lane = lax.broadcasted_iota(jnp.int32, (8, 128), 1)
    inner = lax.bitwise_and(lane, 7)
    planes = []
    for y in range(CY):
        block = slice(8 * y, 8 * y + 8)
        here = own[block, :]
        low = pltpu.roll(before[block, :], 120, 1)
        high = pltpu.roll(after[block, :], 8, 1)
        smooth = GAUSS[0] * here
        for d in range(1, HW + 1):
            ahead = pltpu.roll(jnp.where(inner >= d, here, high), 128 - d, 1)
            behind = pltpu.roll(jnp.where(inner < 8 - d, here, low), d, 1)
            smooth = smooth + GAUSS[d] * (ahead + behind)
        planes.append(smooth)
    rows = out.shape[0]
    for j in range(rows):
        out[j] = jnp.zeros((8, 128), jnp.float32)
    start = coords[1] * CY
    for r in range(-HW, CY + HW):
        mixed = jnp.zeros((8, 128), jnp.float32)
        for y in range(CY):
            if abs(r - y) <= HW:
                mixed = mixed + GAUSS[abs(r - y)] * planes[y]

        @pl.when(jnp.logical_and(start + r >= 0, start + r < rows))
        def _():
            out[start + r] = mixed


def energy_kernel(parts, energy, out):
    lane = lax.broadcasted_iota(jnp.int32, (8, 128), 1)
    sums = energy[0]
    for i in range(1, energy.shape[0]):
        sums = sums + energy[i]
    sums = jnp.where(lane == 8 * COMPS, jnp.sum(sums, axis=1, keepdims=True), 0.0)
    for j in range(out.shape[0]):
        out[j] = parts[j] + sums


def line_kernel(parts, stress, motion, energies):
    count = parts.shape[0] // 8
    lane = lax.broadcasted_iota(jnp.int32, (8, 128), 1)
    sub = lax.broadcasted_iota(jnp.int32, (8, 128), 0)
    lines = []
    for block in range(8):
        line = parts[block]
        for other in range(1, count):
            line = line + parts[8 * other + block]
        lines.append(line)
    whole = lines[0]
    for line in lines[1:]:
        whole = whole + line
    for i in range(3):
        energies[i] = jnp.sum(jnp.where(jnp.logical_and(sub == i, lane == 8 * COMPS), whole, 0.0))
    empty = jnp.zeros((8, 128), jnp.float32)
    out = []
    for block in range(8):
        here = lines[block]
        low = lines[block - 1] if block > 0 else empty
        high = lines[block + 1] if block < 7 else empty
        smooth = GAUSS[0] * here
        for d in range(1, HW + 1):
            ahead = pltpu.roll(jnp.where(sub >= d, here, high), 8 - d, 0)
            behind = pltpu.roll(jnp.where(sub < 8 - d, here, low), d, 0)
            smooth = smooth + GAUSS[d] * (ahead + behind)
        out.append(smooth)
    turned = jnp.concatenate(out, axis=0).T
    for c in range(6):
        stress[c] = turned[8 * c : 8 * c + 8, :]
    for c in range(4):
        motion[c] = turned[48 + 8 * c : 56 + 8 * c, :]


def pack_kernel(*refs):
    sources, (out, to_left, to_right, notes), held, done = refs[0:7], refs[7:11], refs[11:18], refs[18]
    copies = [pltpu.make_async_copy(a, b, done.at[i]) for i, (a, b) in enumerate(zip(sources, held))]
    for copy in copies:
        copy.start()
    for copy in copies:
        copy.wait()
    place, speed, radius, group, broken, lists, counts = held
    code = jnp.where(broken[...] == 0, group[...].astype(jnp.float32), -1.0)
    for t in range(NT):
        for axis in range(3):
            out[t, axis : axis + 1, :] = place[axis, t : t + 1, :]
            out[t, 3 + axis : 4 + axis, :] = speed[axis, t : t + 1, :]
        out[t, 6:7, :] = radius[t : t + 1, :]
        out[t, 7:8, :] = code[t : t + 1, :]
    notes[...] = jnp.zeros((8, 128), jnp.float32)
    for slot in range(K):
        notes[slot : slot + 1, 1 : NT + 1] = lists[0, 0, slot].astype(jnp.float32)
    notes[K : K + 1, 1 : NT + 1] = counts[...].astype(jnp.float32)
    for ref, first in ((to_left, 0), (to_right, NT - 2)):
        ref[0] = out[first]
        ref[1] = out[first + 1]
        ref[2] = notes[...]


def keep_kernel(own, notes, own_out, notes_out):
    own_out[...] = own[...]
    notes_out[...] = notes[...]


def join_kernel(left, own, right, mine, line, notes):
    for i in range(2):
        line[i] = left[i]
        line[NT + 2 + i] = right[i]
    for t in range(NT):
        line[2 + t] = own[t]
    lane = lax.broadcasted_iota(jnp.int32, (8, 128), 1)
    edges = jnp.where(lane == 0, pltpu.roll(left[2], 128 - NT, 1), pltpu.roll(right[2], NT, 1))
    notes[...] = jnp.where(jnp.logical_and(lane >= 1, lane <= NT), mine[...], edges)


def shifted(value, axis, step, wrap):
    count = lax.axis_size(axis)
    pairs = [(i, (i + step) % count) for i in range(count) if wrap or 0 <= i + step < count]
    return lax.ppermute(value, axis, pairs)


def list_entries(lists, counts, home, shift, width, margin):
    offset = lists // NT
    along = offset // 9 - 1
    across = offset // 3 % 3
    up = offset % 3
    spot = jnp.clip((along + shift) * NT + lists % NT + margin, 0, width - 1)

    def within(axis, step):
        moved = lax.axis_index(axis) + step
        return (moved >= 0) & (moved < lax.axis_size(axis))

    slot = lax.broadcasted_iota(jnp.int32, lists.shape, 0)
    live = (slot < counts) & within("gx", shift) & within("gx", shift + along)
    live = live & within("gy", across - 1) & within("gz", up - 1)
    inside = live & (offset == 13)
    itself = inside & (spot == home)
    entry = up * (3 * width) + across * width + spot
    entry = entry + LIVE * live.astype(jnp.int32) + INSIDE * inside.astype(jnp.int32)
    entry = entry + ITSELF * itself.astype(jnp.int32)
    own = inside.astype(jnp.int32)
    earlier = lax.broadcasted_iota(jnp.int32, (K, K, 1), 0) < lax.broadcasted_iota(jnp.int32, (K, K, 1), 1)
    before = jnp.sum(jnp.where(earlier, own[:, None, :], 0), axis=0)
    rank = jnp.where(inside, before, slot - before + jnp.sum(own, axis=0, keepdims=True))
    to = lax.broadcasted_iota(jnp.int32, (1, K, 1), 1)
    return jnp.sum(jnp.where(rank[:, None, :] == to, entry[:, None, :], 0), axis=0).reshape(-1)


def shards(positions, velocities, radius, group, broken, cell, neighbours, counts):
    tile = jax.ShapeDtypeStruct((NT, 8, 128), jnp.float32)
    edge = jax.ShapeDtypeStruct((3, 8, 128), jnp.float32)
    arguments = (
        positions.reshape(3, NT, 128),
        velocities.reshape(3, NT, 128),
        radius.reshape(NT, 128),
        group.reshape(NT, 128),
        broken.reshape(NT, 128),
        jnp.transpose(neighbours, (0, 1, 4, 2, 3)),
        counts.reshape(1, NT),
    )
    own, to_left, to_right, notes = pl.pallas_call(
        pack_kernel,
        out_shape=(tile, edge, edge, jax.ShapeDtypeStruct((8, 128), jnp.float32)),
        in_specs=[pl.BlockSpec(memory_space=pltpu.HBM)] * 7,
        out_specs=(VMEM,) * 4,
        scratch_shapes=[pltpu.VMEM(a.shape, a.dtype) for a in arguments] + [pltpu.SemaphoreType.DMA((7,))],
        name="pack",
    )(*arguments)
    own, notes = pl.pallas_call(
        keep_kernel,
        out_shape=(tile, jax.ShapeDtypeStruct((8, 128), jnp.float32)),
        in_specs=[VMEM] * 2,
        out_specs=(VMEM,) * 2,
        compiler_params=SMALL,
        cost_estimate=pl.CostEstimate(flops=0, bytes_accessed=2 << 20, transcendentals=0),
        name="keep",
    )(own, notes)
    from_left = shifted(to_right, "gx", 1, True)
    from_right = shifted(to_left, "gx", -1, True)
    width = NT + 4
    line, listed = pl.pallas_call(
        join_kernel,
        out_shape=(
            jax.ShapeDtypeStruct((width, 8, 128), jnp.float32),
            jax.ShapeDtypeStruct((8, 128), jnp.float32),
        ),
        in_specs=[VMEM] * 4,
        out_specs=(VMEM,) * 2,
        compiler_params=SMALL,
        name="join",
    )(from_left, own, from_right, notes)

    def extended(tiles):
        up = shifted(tiles, "gy", 1, False)
        down = shifted(tiles, "gy", -1, False)
        middle = jnp.concatenate([up, tiles, down], axis=0)
        low = shifted(middle, "gz", 1, True)
        high = shifted(middle, "gz", -1, True)
        return low, middle, high

    low, middle, high = extended(line)
    mine = turned(middle, width - 2)
    listed = listed[0 : K + 1, 0 : NT + 2].astype(jnp.int32)
    spots = lax.broadcasted_iota(jnp.int32, (1, NT + 2), 1)
    shift = jnp.where(spots == 0, -1, jnp.where(spots == NT + 1, 1, 0))
    first_meta = list_entries(listed[0:K], listed[K:], spots + 1, shift, width, 2)
    spots = lax.broadcasted_iota(jnp.int32, (1, NT), 1)
    second_meta = list_entries(listed[0:K, 1 : NT + 1], listed[K:, 1 : NT + 1], spots + 1, 0, width - 2, 1)

    line = pl.pallas_call(
        first_kernel,
        out_shape=jax.ShapeDtypeStruct((width - 2, 8, 128), jnp.float32),
        in_specs=[SMEM] + [VMEM] * 4,
        out_specs=VMEM,
        scratch_shapes=[
            pltpu.VMEM((9 * width, 8, 128), jnp.float32),
            *work_space(),
        ],
        compiler_params=LARGE,
        name="first_step",
    )(first_meta, low, middle, high, mine)
    low, middle, high = extended(line)
    mine = turned(middle, NT)
    width = width - 2
    peers = lax.axis_size("gx")
    block = jax.ShapeDtypeStruct((3, NT, 128), jnp.float32)
    places, speeds, values, energy = pl.pallas_call(
        second_kernel,
        out_shape=(
            block,
            block,
            jax.ShapeDtypeStruct((NT, 16, 128), jnp.float32),
            jax.ShapeDtypeStruct((peers, 8, 128), jnp.float32),
        ),
        in_specs=[SMEM] + [VMEM] * 4,
        out_specs=(VMEM,) * 4,
        scratch_shapes=[
            pltpu.VMEM((9 * width, 8, 128), jnp.float32),
            pltpu.VMEM((8, 128), jnp.float32),
            *work_space(),
        ],
        compiler_params=LARGE,
        name="second_step",
    )(second_meta, low, middle, high, mine)
    energy = lax.all_to_all(energy, "gx", 0, 0, tiled=True)
    grid = pl.pallas_call(
        deposit_kernel,
        out_shape=jax.ShapeDtypeStruct((64, 128), jnp.float32),
        in_specs=[VMEM] * 2,
        out_specs=VMEM,
        scratch_shapes=[
            pltpu.VMEM((64, NT * 128), jnp.bfloat16),
            pltpu.VMEM((256, NT * 128), jnp.bfloat16),
        ],
        compiler_params=SMALL,
        name="deposit",
    )(values, cell.reshape(NT, 128))
    before = shifted(grid, "gx", 1, False)
    after = shifted(grid, "gx", -1, False)
    coords = jnp.stack([lax.axis_index(a) for a in ("gx", "gy", "gz")])
    rows = lax.axis_size("gy") * lax.axis_size("gz")
    parts = pl.pallas_call(
        plane_kernel,
        out_shape=jax.ShapeDtypeStruct((rows, 8, 128), jnp.float32),
        in_specs=[SMEM] + [VMEM] * 3,
        out_specs=VMEM,
        compiler_params=SMALL,
        name="planes",
    )(coords, grid, before, after)
    parts = pl.pallas_call(
        energy_kernel,
        out_shape=jax.ShapeDtypeStruct((rows, 8, 128), jnp.float32),
        in_specs=[VMEM] * 2,
        out_specs=VMEM,
        compiler_params=SMALL,
        name="energies",
    )(parts, energy)
    parts = lax.all_to_all(parts, ("gy", "gz"), 0, 0, tiled=True)
    stress, motion, energies = pl.pallas_call(
        line_kernel,
        out_shape=(
            jax.ShapeDtypeStruct((6, 8, 64), jnp.float32),
            jax.ShapeDtypeStruct((4, 8, 64), jnp.float32),
            jax.ShapeDtypeStruct((3,), jnp.float32),
        ),
        in_specs=[VMEM],
        out_specs=(VMEM, VMEM, SMEM),
        compiler_params=SMALL,
        name="lines",
    )(parts)
    return (
        places.reshape(positions.shape),
        speeds.reshape(velocities.shape),
        stress.reshape(6, CX, 1, 64),
        motion.reshape(4, CX, 1, 64),
        energies,
    )


def solution(mesh):
    placed = (
        P(None, "gx", "gy", "gz", None),
        P(None, "gx", "gy", "gz", None),
        P("gx", "gy", "gz", None),
        P("gx", "gy", "gz", None),
        P("gx", "gy", "gz", None),
        P("gx", "gy", "gz", None),
        P("gx", "gy", "gz", None, None),
        P("gx", "gy", "gz", None),
    )
    return jax.shard_map(
        shards,
        mesh=mesh,
        in_specs=placed,
        out_specs=(
            P(None, "gx", "gy", "gz", None),
            P(None, "gx", "gy", "gz", None),
            P(None, "gx", ("gy", "gz"), None),
            P(None, "gx", ("gy", "gz"), None),
            P(),
        ),
        check_vma=False,
    )
```
